32 devices in a mesh: sens: 16 (over z, x, core), hour: 2 (over y).
Axes of the slice: x: 2, y: 2, z: 4, core: 2. Of those that a mesh axis runs over, the one named last changes fastest.
Arguments:
- windows: bfloat16 [2, 128, 3, 4096], P('hour', 'sens'), may hold values from -6 to 6
- pair_first: int32 [1024], P('sens'), may hold values from 0 to 7
- pair_second: int32 [1024], P('sens'), may hold values from 0 to 23
- owners: int32 [1024, 1], P('sens'), may hold values from 0 to 15; in each aligned block of 64 rows (0 to 63, 64 to 127, ...) at most 8 rows name the same one
Outputs:
- stacks: float32 [2048, 9216], P('sens', 'hour')
The draws below stay inside these ranges and needn't reach their ends.
Inputs may be any that keep to these rules, and one draw needn't show every extreme that they name: `owners`: within the 64 pairs of one block no owner appears more than 8 times, and some owner appears exactly 8 times.
All inputs are finite; a program needn't handle non-finite values.
Results may differ from the reference program's by a relative error of at most 0.004.
Values may be sent and summed in bfloat16 or wider, within the bound.
A program may use at most 128 MiB of HBM per device.

```python
import math
import jax
import jax.numpy as jnp
import numpy as np
from jax import lax

SAMPLES = 4096
PADDED = 8192
NB = 2048
LAGS = 1024
COMPS = 3
S_DEV = 8
PAIRS_DEV = 64
CAP = 8
SENSORS = 128
HOURS = 2
PAIR_ROWS = 1024
SLOTS = 2048
N_SENS = 16


def touch_ends(entries, own_key, smallest, high):
    place = [jax.random.randint(jax.random.fold_in(own_key, axis), (), 0, length) for axis, length in enumerate(entries.shape)]
    longest = entries.shape.index(max(entries.shape))
    neighbour = place[:longest] + [(place[longest] + 1) % entries.shape[longest]] + place[longest + 1:]
    return entries.at[tuple(place)].set(smallest).at[tuple(neighbour)].set(high)


def shard_levels(stream_key, extent, split, smallest, high):
    factor_of, own = 1.0, jax.random.fold_in(stream_key, 6)
    for position, parts in split:
        steps = jnp.exp(jax.random.uniform(jax.random.fold_in(own, position), (parts,), jnp.float32, smallest / len(split), high / len(split)))
        factor_of = factor_of * jnp.repeat(steps, extent[position] // parts).reshape([-1 if axis == position else 1 for axis in range(len(extent))])
    return factor_of


def routed_block(stream_key, own, number, rows, number_of, top, limit, lean):
    order = jax.random.permutation(stream_key, number_of)
    crowded, usual = shares(number_of, rows * top, limit, lean, True), shares(number_of, rows * top, limit, lean, False)
    places = jnp.arange(number_of)

    def named(tallies, rotation):
        used = int((tallies > 0).sum())
        fixed = max(1, used // 4)
        shifted = fixed + (places - fixed + rotation * (used - fixed)) % max(1, number_of - fixed)
        return jnp.zeros((number_of,), jnp.int32).at[order[jnp.where(places < fixed, places, shifted)]].set(jnp.asarray(tallies, jnp.int32))

    tallies = jnp.where(number % 4 == 0, named(crowded, number // 4), named(usual, number - number // 4 - 1))
    mixed = jax.random.permutation(jax.random.fold_in(own, 3), number_of)
    source_of, receiver = mixed[0:number_of // 2 * 2:2], mixed[1:number_of // 2 * 2:2]
    room = jnp.minimum(tallies[source_of] - 1, limit - tallies[receiver]) // 2
    room = jnp.where((source_of == order[0]) | (receiver == order[0]) | (tallies[receiver] == 0), 0, jnp.maximum(room, 0))
    shifted = jax.random.randint(jax.random.fold_in(own, 4), (number_of // 2,), 0, 1 << 20) % (room + 1)
    tallies = tallies.at[source_of].add(-shifted).at[receiver].add(shifted)
    members = jnp.searchsorted(jnp.cumsum(tallies), jnp.arange(rows * top), side="right").astype(jnp.int32)
    table = members.reshape(top, rows).T
    table = table[jax.random.permutation(jax.random.fold_in(own, 1), rows)]
    rotation = jax.random.randint(jax.random.fold_in(own, 2), (rows, 1), 0, top)
    return jnp.take_along_axis(table, (jnp.arange(top)[None, :] + rotation) % top, axis=1)


def shares(count, total, reach, skew, full):
    weights = [(1 << 20) // math.isqrt(standing ** skew) + 1 for standing in range(1, count + 1)]
    largest = reach if full else min(reach, max(-(-total // count), total * weights[0] // sum(weights)))
    least = 1 if total - largest >= count - 1 else 0
    counts, spare = [largest] + [least] * (count - 1), total - largest - least * (count - 1)
    while spare > 0:
        movable = [i for i in range(1, count) if counts[i] < largest] or [i for i in range(1, count) if counts[i] < reach]
        pool, budget = sum([weights[i] for i in movable]), spare
        for i in movable:
            more = min(reach - counts[i], max(1, budget * weights[i] // pool), spare)
            counts[i] = counts[i] + more
            spare = spare - more
    return np.array(counts)


def scatter_about(own_key, dims, scale, limit, split=(), kind=jnp.bfloat16):
    level = shard_levels(own_key, dims, split, -0.22, 0.18) if split else 1.0
    result = jax.random.normal(own_key, dims, jnp.float32) * scale * level
    return jnp.minimum(jnp.maximum(result, -limit), limit).astype(kind)


def setup_inputs(seed: int = 0) -> dict:
    keys = jax.random.split(jax.random.key(seed), 5)
    windows = scatter_about(keys[0], (HOURS, SENSORS, COMPS, SAMPLES), 1.0, 6.0, ((0, 2), (1, 16)))
    pair_first = touch_ends(jax.random.randint(keys[1], (PAIR_ROWS,), 0, S_DEV), jax.random.fold_in(keys[1], 1), 0, S_DEV - 1).astype(jnp.int32)
    pair_second = touch_ends(jax.random.randint(keys[2], (PAIR_ROWS,), 0, 3 * S_DEV), jax.random.fold_in(keys[2], 1), 0, (3 * S_DEV) - 1).astype(jnp.int32)
    owners_keys = jax.random.split(jax.random.fold_in(keys[3], 1), PAIR_ROWS // PAIRS_DEV)
    owners_turns = jax.random.permutation(jax.random.fold_in(keys[3], 3), PAIR_ROWS // PAIRS_DEV)
    owners = jax.vmap(lambda own, number: routed_block(jax.random.fold_in(keys[3], 2), own, number, PAIRS_DEV, N_SENS, 1, CAP, 2))(owners_keys, owners_turns).reshape((PAIR_ROWS, 1))
    return {"windows": windows, "pair_first": pair_first, "pair_second": pair_second, "owners": owners}


def build_tables():
    times = jnp.arange(SAMPLES, dtype=jnp.int32)
    bins = jnp.arange(NB, dtype=jnp.int32) + 1
    phase = times[:, None] * bins[None, :] % PADDED
    angle = phase.astype(jnp.float32) * (2.0 * jnp.pi / PADDED)
    fwd = jnp.concatenate([jnp.cos(angle), -jnp.sin(angle)], axis=1).astype(jnp.bfloat16)
    shifts = jnp.arange(LAGS, dtype=jnp.int32) - LAGS // 2
    phase_back = bins[:, None] * shifts[None, :] % PADDED
    angle_back = phase_back.astype(jnp.float32) * (2.0 * jnp.pi / PADDED)
    inv = jnp.concatenate([jnp.cos(angle_back), -jnp.sin(angle_back)], axis=0).astype(jnp.bfloat16)
    return (fwd, inv)

def whiten(rows, fwd):
    spec = jnp.dot(rows, fwd, preferred_element_type=jnp.float32)
    real_part = spec[:, :NB]
    imag_part = spec[:, NB:]
    power = real_part * real_part + imag_part * imag_part
    level = lax.optimization_barrier(jnp.mean(power, axis=1, keepdims=True))
    scale = 1.0 / jnp.sqrt(power + 0.1 * level + 1e-06)
    return jnp.concatenate([real_part * scale, imag_part * scale], axis=1).astype(jnp.bfloat16)

def correlate(first_spec, second_spec, inv):
    ar = first_spec[..., :NB].astype(jnp.float32)
    ai = first_spec[..., NB:].astype(jnp.float32)
    br = second_spec[..., :NB].astype(jnp.float32)
    bi = second_spec[..., NB:].astype(jnp.float32)
    real_part = ar[:, :, None, :] * br[:, None, :, :] + ai[:, :, None, :] * bi[:, None, :, :]
    imag_part = ar[:, :, None, :] * bi[:, None, :, :] - ai[:, :, None, :] * br[:, None, :, :]
    cross = jnp.concatenate([real_part, imag_part], axis=-1).astype(jnp.bfloat16)
    count = cross.shape[0]
    lagged = jnp.dot(cross.reshape(count * COMPS * COMPS, 2 * NB), inv, preferred_element_type=jnp.float32)
    return lagged.reshape(count, COMPS * COMPS * LAGS)

def reference(windows, pair_first, pair_second, owners):
    fwd, inv = build_tables()

    def one_hour(hour_windows):
        rows = hour_windows.reshape(SENSORS * COMPS, SAMPLES)
        return whiten(rows, fwd).reshape(SENSORS, COMPS, 2 * NB)
    white = lax.map(one_hour, windows)
    rows_index = jnp.arange(PAIR_ROWS, dtype=jnp.int32)
    block = rows_index // PAIRS_DEV
    sensor_a = block * S_DEV + pair_first
    sensor_b = (block + pair_second // S_DEV) % N_SENS * S_DEV + pair_second % S_DEV

    def add_hour(total, hour_white):
        return (total + correlate(hour_white[sensor_a], hour_white[sensor_b], inv), None)
    start = jnp.zeros((PAIR_ROWS, COMPS * COMPS * LAGS), jnp.float32)
    summed, _ = lax.scan(add_hour, start, white)
    stack = summed / jnp.sqrt(jnp.float32(NB * HOURS))
    owner = owners[:, 0].reshape(N_SENS, PAIRS_DEV)
    same = owner[:, :, None] == owner[:, None, :]
    order = jnp.arange(PAIRS_DEV, dtype=jnp.int32)
    earlier = order[None, :] < order[:, None]
    slot = lax.optimization_barrier(jnp.sum((same & earlier[None, :, :]).astype(jnp.int32), axis=2)).reshape(PAIR_ROWS)
    target = owners[:, 0] * (N_SENS * CAP) + block * CAP + slot
    stacks = jnp.zeros((SLOTS, COMPS * COMPS * LAGS), jnp.float32).at[target].set(stack)
    return stacks
```

```python
import jax
import jax.numpy as jnp
import ml_dtypes
import numpy as np
from jax import lax
from jax.sharding import PartitionSpec as P

SAMPLES = 4096
PADDED = 8192
NB = 2048
LAGS = 1024
COMPS = 3
WIDTH = COMPS * COMPS * LAGS
HALF = SAMPLES // 2


def host_tables():
    times = np.arange(HALF, dtype=np.int64)
    bins = np.arange(NB, dtype=np.int64) + 1
    angle = (times[:, None] * bins[None, :] % PADDED) * (2.0 * np.pi / PADDED)
    fwd = np.concatenate([np.cos(angle), -np.sin(angle)], axis=1).astype(ml_dtypes.bfloat16)
    shifts = np.arange(LAGS, dtype=np.int64) - LAGS // 2
    back = (bins[:, None] * shifts[None, :] % PADDED) * (2.0 * np.pi / PADDED)
    inv = np.concatenate([np.cos(back), -np.sin(back)], axis=0).astype(ml_dtypes.bfloat16)
    return fwd, inv


def whiten(rows, fwd):
    count = rows.shape[0]
    both = jnp.concatenate([rows[:, :HALF], rows[:, HALF:]], axis=0)
    spec = jnp.dot(both, fwd, preferred_element_type=jnp.float32)
    ar, ai = spec[:count, :NB], spec[:count, NB:]
    br, bi = spec[count:, :NB], spec[count:, NB:]
    turn = (lax.broadcasted_iota(jnp.int32, (1, NB), 1) + 1) % 4
    even = turn % 2 == 0
    sign_re = jnp.where((turn == 0) | (turn == 1), 1.0, -1.0)
    sign_im = jnp.where((turn == 0) | (turn == 3), 1.0, -1.0)
    real_part = ar + sign_re * jnp.where(even, br, bi)
    imag_part = ai + sign_im * jnp.where(even, bi, br)
    power = real_part * real_part + imag_part * imag_part
    level = jnp.mean(power, axis=1, keepdims=True)
    scale = 1.0 / jnp.sqrt(power + 0.1 * level + 1e-06)
    return jnp.concatenate([real_part * scale, imag_part * scale], axis=1).astype(jnp.bfloat16)


def from_behind(value, axis, steps):
    count = lax.axis_size(axis)
    pairs = [(source, (source + steps) % count) for source in range(count)]
    return lax.ppermute(value, axis, pairs)


def pick(rows, index):
    table = (index[:, None] == jnp.arange(rows.shape[0], dtype=jnp.int32)[None, :]).astype(jnp.bfloat16)
    return jnp.dot(table, rows, preferred_element_type=jnp.float32)


def shards(windows, pair_first, pair_second, owners):
    hours_here, sensors, _, _ = windows.shape
    pairs = pair_first.shape[0]
    hour_count = lax.axis_size("hour")
    owner_count = lax.axis_size("sens")
    hours = hours_here * hour_count
    columns = WIDTH // hour_count
    capacity = max(2, 2 * pairs // owner_count)
    fwd, inv = (jnp.asarray(table) for table in host_tables())

    white = whiten(windows.reshape(hours_here * sensors * COMPS, SAMPLES), fwd)
    white = lax.all_gather(white, "hour", axis=0, tiled=True)
    white = white.reshape(hours, sensors, COMPS * 2 * NB)
    nearer = from_behind(white, "sens", -1)
    farther = from_behind(white, "sens", -2)
    candidates = jnp.concatenate([white, nearer, farther], axis=1)

    start = lax.axis_index("hour") * columns
    first_block = start // LAGS
    blocks = min(COMPS * COMPS, max((h * columns + columns - 1) // LAGS - h * columns // LAGS + 1 for h in range(hour_count)))
    first_block = jnp.minimum(first_block, COMPS * COMPS - blocks)
    kinds = first_block + jnp.arange(blocks, dtype=jnp.int32)

    total_re, total_im = 0.0, 0.0
    for hour in range(hours):
        a = pick(white[hour], pair_first).reshape(pairs, COMPS, 2, NB)
        b = pick(candidates[hour], pair_second).reshape(pairs, COMPS, 2, NB)
        a = jnp.take(a, kinds // COMPS, axis=1)
        b = jnp.take(b, kinds % COMPS, axis=1)
        ar, ai, br, bi = a[:, :, 0], a[:, :, 1], b[:, :, 0], b[:, :, 1]
        total_re = total_re + (ar * br + ai * bi)
        total_im = total_im + (ar * bi - ai * br)
    cross = jnp.concatenate([total_re, total_im], axis=-1).astype(jnp.bfloat16)
    lagged = jnp.dot(cross.reshape(pairs * blocks, 2 * NB), inv, preferred_element_type=jnp.float32)
    lagged = lagged.astype(jnp.bfloat16).reshape(pairs, blocks * LAGS)
    lagged = lax.dynamic_slice_in_dim(lagged, start - first_block * LAGS, columns, axis=1)

    owner = owners[:, 0]
    order = jnp.arange(pairs, dtype=jnp.int32)
    earlier = (owner[:, None] == owner[None, :]) & (order[None, :] < order[:, None])
    target = owner * capacity + jnp.sum(earlier.astype(jnp.int32), axis=1)
    place = (jnp.arange(owner_count * capacity, dtype=jnp.int32)[:, None] == target[None, :]).astype(jnp.bfloat16)
    outgoing = jnp.dot(place, lagged, preferred_element_type=jnp.float32).astype(jnp.bfloat16)
    received = lax.all_to_all(outgoing, "sens", split_axis=0, concat_axis=0, tiled=True)
    return received.astype(jnp.float32) / jnp.sqrt(jnp.float32(NB * hours))


def solution(mesh):
    placed = (P("hour", "sens", None, None), P("sens"), P("sens"), P("sens", None))
    return jax.shard_map(
        shards, mesh=mesh, in_specs=placed, out_specs=P("sens", "hour"), check_vma=False
    )
```

```python
import functools

import jax
import jax.numpy as jnp
import ml_dtypes
import numpy as np
from jax import lax
from jax.experimental import pallas as pl
from jax.experimental.pallas import tpu as pltpu
from jax.sharding import PartitionSpec as P

SAMPLES = 4096
PADDED = 8192
NB = 2048
LAGS = 1024
COMPS = 3
WIDTH = COMPS * COMPS * LAGS
HALF = SAMPLES // 2
QUARTER = NB // 2
BLOCK = 128
CHUNKS = QUARTER // BLOCK
MESH = pl.DeviceIdType.MESH
F32 = jnp.float32
BF16 = jnp.bfloat16

def host_tables():
    times = np.arange(HALF, dtype=np.int64)
    bins = np.arange(NB, dtype=np.int64) + 1
    angle = (times[:, None] * bins[None, :] % PADDED) * (2.0 * np.pi / PADDED)
    fwd = np.concatenate([np.cos(angle), -np.sin(angle)], axis=1).astype(ml_dtypes.bfloat16)
    shifts = np.arange(LAGS, dtype=np.int64) - LAGS // 2
    back = (bins[:, None] * shifts[None, :] % PADDED) * (2.0 * np.pi / PADDED)
    inv = np.concatenate([np.cos(back), -np.sin(back)], axis=0).astype(ml_dtypes.bfloat16)
    return fwd, inv


def whiten(rows, fwd):
    count = rows.shape[0]
    both = jnp.concatenate([rows[:, :HALF], rows[:, HALF:]], axis=0)
    spec = jnp.dot(both, fwd, preferred_element_type=jnp.float32)
    ar, ai = spec[:count, :NB], spec[:count, NB:]
    br, bi = spec[count:, :NB], spec[count:, NB:]
    turn = (lax.broadcasted_iota(jnp.int32, (1, NB), 1) + 1) % 4
    even = turn % 2 == 0
    sign_re = jnp.where((turn == 0) | (turn == 1), 1.0, -1.0)
    sign_im = jnp.where((turn == 0) | (turn == 3), 1.0, -1.0)
    real_part = ar + sign_re * jnp.where(even, br, bi)
    imag_part = ai + sign_im * jnp.where(even, bi, br)
    power = real_part * real_part + imag_part * imag_part
    level = jnp.mean(power, axis=1, keepdims=True)
    scale = 1.0 / jnp.sqrt(power + 0.1 * level + 1e-06)
    return jnp.concatenate([real_part * scale, imag_part * scale], axis=1).astype(jnp.bfloat16)


def from_behind(value, axis, steps):
    count = lax.axis_size(axis)
    pairs = [(source, (source + steps) % count) for source in range(count)]
    return lax.ppermute(value, axis, pairs)


def pick(rows, index):
    table = (index[:, None] == jnp.arange(rows.shape[0], dtype=jnp.int32)[None, :]).astype(jnp.bfloat16)
    return jnp.dot(table, rows, preferred_element_type=jnp.float32)


def plain_shards(windows, pair_first, pair_second, owners):
    hours_here, sensors, _, _ = windows.shape
    pairs = pair_first.shape[0]
    hour_count = lax.axis_size("hour")
    owner_count = lax.axis_size("sens")
    hours = hours_here * hour_count
    columns = WIDTH // hour_count
    capacity = max(2, 2 * pairs // owner_count)
    fwd, inv = (jnp.asarray(table) for table in host_tables())

    white = whiten(windows.reshape(hours_here * sensors * COMPS, SAMPLES), fwd)
    white = lax.all_gather(white, "hour", axis=0, tiled=True)
    white = white.reshape(hours, sensors, COMPS * 2 * NB)
    nearer = from_behind(white, "sens", -1)
    farther = from_behind(white, "sens", -2)
    candidates = jnp.concatenate([white, nearer, farther], axis=1)

    start = lax.axis_index("hour") * columns
    first_block = start // LAGS
    blocks = min(COMPS * COMPS, max((h * columns + columns - 1) // LAGS - h * columns // LAGS + 1 for h in range(hour_count)))
    first_block = jnp.minimum(first_block, COMPS * COMPS - blocks)
    kinds = first_block + jnp.arange(blocks, dtype=jnp.int32)

    total_re, total_im = 0.0, 0.0
    for hour in range(hours):
        a = pick(white[hour], pair_first).reshape(pairs, COMPS, 2, NB)
        b = pick(candidates[hour], pair_second).reshape(pairs, COMPS, 2, NB)
        a = jnp.take(a, kinds // COMPS, axis=1)
        b = jnp.take(b, kinds % COMPS, axis=1)
        ar, ai, br, bi = a[:, :, 0], a[:, :, 1], b[:, :, 0], b[:, :, 1]
        total_re = total_re + (ar * br + ai * bi)
        total_im = total_im + (ar * bi - ai * br)
    cross = jnp.concatenate([total_re, total_im], axis=-1).astype(jnp.bfloat16)
    lagged = jnp.dot(cross.reshape(pairs * blocks, 2 * NB), inv, preferred_element_type=jnp.float32)
    lagged = lagged.astype(jnp.bfloat16).reshape(pairs, blocks * LAGS)
    lagged = lax.dynamic_slice_in_dim(lagged, start - first_block * LAGS, columns, axis=1)

    owner = owners[:, 0]
    order = jnp.arange(pairs, dtype=jnp.int32)
    earlier = (owner[:, None] == owner[None, :]) & (order[None, :] < order[:, None])
    target = owner * capacity + jnp.sum(earlier.astype(jnp.int32), axis=1)
    place = (jnp.arange(owner_count * capacity, dtype=jnp.int32)[:, None] == target[None, :]).astype(jnp.bfloat16)
    outgoing = jnp.dot(place, lagged, preferred_element_type=jnp.float32).astype(jnp.bfloat16)
    received = lax.all_to_all(outgoing, "sens", split_axis=0, concat_axis=0, tiled=True)
    return received.astype(jnp.float32) / jnp.sqrt(jnp.float32(NB * hours))


def folded_tables():
    times = np.arange(HALF, dtype=np.int64)
    bins = np.arange(QUARTER, dtype=np.int64)
    angle = (times[:, None] * bins[None, :] % PADDED) * (2.0 * np.pi / PADDED)
    cosine, sine = np.cos(angle), np.sin(angle)
    sine[:, 0] = 1 - 2 * (times // 4 % 2)
    both = np.stack([cosine.reshape(HALF, CHUNKS, BLOCK), sine.reshape(HALF, CHUNKS, BLOCK)], axis=2)
    fwd = both.transpose(1, 0, 2, 3).reshape(CHUNKS, HALF, 2 * BLOCK).astype(ml_dtypes.bfloat16)
    order = np.concatenate([bins, NB - bins])
    order[0] = QUARTER
    shifts = np.arange(LAGS, dtype=np.int64) - LAGS // 2
    back = (order[:, None] * shifts[None, :] % PADDED) * (2.0 * np.pi / PADDED)
    inv = np.concatenate([np.cos(back), -np.sin(back)], axis=0)
    inv = inv.reshape(2 * NB, 4, LAGS // 4).transpose(1, 0, 2).astype(ml_dtypes.bfloat16)
    return fwd, inv


def kernel(
    n, pairs, x_ref, first_ref, second_ref, owner_col_ref, owner_row_ref, fwd_hbm, inv_hbm, out_ref,
    fwd_v, inv_v, xm, spec, white, a_v, b_v, cross, lagged, outgoing,
    fwd_sem, inv_sem, near_send, near_recv, far_send, far_recv, own_sem,
):
    me = lax.axis_index("sens")
    hour = lax.axis_index("hour")
    other = 1 - hour

    barrier = pltpu.get_barrier_semaphore()

    def greet(step, carry):
        pl.semaphore_signal(barrier, inc=1, device_id=(lax.rem(me + step, n), hour), device_id_type=MESH)
        return carry

    lax.fori_loop(1, n, greet, 0)
    pl.semaphore_signal(barrier, inc=1, device_id=(me, other), device_id_type=MESH)

    def fwd_copy(c):
        return pltpu.make_async_copy(fwd_hbm.at[c], fwd_v.at[c], fwd_sem.at[c])

    def inv_copy(c):
        return pltpu.make_async_copy(inv_hbm.at[c], inv_v.at[c], inv_sem.at[c])

    for c in range(CHUNKS):
        fwd_copy(c).start()
    for c in range(4):
        inv_copy(c).start()

    rows = x_ref.shape[0]
    x = x_ref[...].astype(F32)
    halves = jnp.concatenate([x[:, :HALF], x[:, HALF:]], axis=0)
    residue = lax.broadcasted_iota(jnp.int32, (2 * rows, HALF), 1) & 3
    xm[...] = jnp.concatenate([jnp.where(residue == r, halves, 0.0) for r in range(4)], axis=0).astype(BF16)

    lane = lax.broadcasted_iota(jnp.int32, (rows, BLOCK), 1)
    turn = lane & 3
    root = 0.70703125

    def transform(c, total):
        fwd_copy(c).wait()
        part = jnp.dot(xm[...], fwd_v[c], preferred_element_type=F32)
        pc, ps = [], []
        for r in range(4):
            top = part[2 * r * rows:(2 * r + 1) * rows]
            low = part[(2 * r + 1) * rows:(2 * r + 2) * rows]
            c1, s1 = low[:, :BLOCK], low[:, BLOCK:]
            pc.append(top[:, :BLOCK] + jnp.where(turn == 0, c1, jnp.where(turn == 1, -s1, jnp.where(turn == 2, -c1, s1))))
            ps.append(top[:, BLOCK:] + jnp.where(turn == 0, s1, jnp.where(turn == 1, c1, jnp.where(turn == 2, -s1, -c1))))
        ends = (lane == 0) & (c == 0)
        re_a = jnp.where(ends, ps[0] + root * (ps[1] - ps[3]), pc[0] + pc[1] + pc[2] + pc[3])
        im_a = -jnp.where(ends, ps[2] + root * (ps[1] + ps[3]), ps[0] + ps[1] + ps[2] + ps[3])
        zero_sine = jnp.where(ends, 0.0, 1.0)
        re_b = pc[0] - pc[2] + zero_sine * (ps[1] - ps[3])
        im_b = pc[3] - pc[1] + zero_sine * (ps[0] - ps[2])
        near = pl.ds(pl.multiple_of(c * BLOCK, BLOCK), BLOCK)
        far = pl.ds(pl.multiple_of(QUARTER + c * BLOCK, BLOCK), BLOCK)
        spec[0, :, near] = re_a
        spec[0, :, far] = re_b
        spec[1, :, near] = im_a
        spec[1, :, far] = im_b
        return total + (re_a * re_a + im_a * im_a) + (re_b * re_b + im_b * im_b)

    total = lax.fori_loop(0, CHUNKS, transform, jnp.zeros((rows, BLOCK), F32))
    level = jnp.sum(total, axis=1, keepdims=True) * (1.0 / NB)
    real_part, imag_part = spec[0], spec[1]
    scale = 1.0 / jnp.sqrt(real_part * real_part + imag_part * imag_part + 0.1 * level + 1e-06)
    white[0, 0] = jnp.concatenate([real_part * scale, imag_part * scale], axis=0).astype(BF16)

    pl.semaphore_wait(barrier, n)
    even = lax.rem(me, 2) == 0
    odd = lax.rem(me, 2) == 1
    behind = (lax.rem(me + n - 1, n), hour)
    behind2 = (lax.rem(me + n - 2, n), hour)
    ahead = (lax.rem(me + 1, n), hour)
    across = (me, other)

    def near_copy(src, dst, send, recv, device):
        return pltpu.make_async_remote_copy(
            src_ref=white.at[src[0], src[1]], dst_ref=white.at[dst[0], dst[1]],
            send_sem=near_send.at[send], recv_sem=near_recv.at[recv], device_id=device, device_id_type=MESH,
        )

    copy_far = near_copy((0, 0), (0, 2), 0, 0, behind2)
    copy_hour = near_copy((0, 0), (1, 0), 1, 1, across)
    copy_both = near_copy((0, 2), (1, 2), 2, 2, across)
    odd_own = near_copy((0, 0), (0, 1), 3, 3, behind)
    even_own = near_copy((0, 2), (0, 1), 3, 3, ahead)
    odd_other = near_copy((1, 0), (1, 1), 4, 4, behind)
    even_other = near_copy((1, 2), (1, 1), 4, 4, ahead)

    copy_far.start()
    copy_hour.start()

    @pl.when(odd)
    def _():
        odd_own.start()

    copy_far.wait_recv()
    copy_both.start()

    @pl.when(even)
    def _():
        even_own.start()

    copy_hour.wait_recv()

    @pl.when(odd)
    def _():
        odd_other.start()

    half_rows = rows
    group = 2 * rows
    wide = lax.broadcasted_iota(jnp.int32, (pairs, 3 * group), 1)
    first, second = first_ref[...], second_ref[...]
    second_base = second // 8 * group + second % 8 * COMPS
    pick_a, pick_b = [], []
    for part in range(2):
        for comp in range(COMPS):
            shift = part * half_rows + comp
            pick_a.append(jnp.where(wide[:, :group] == first * COMPS + shift, 1.0, 0.0))
            pick_b.append(jnp.where(wide == second_base + shift, 1.0, 0.0))
    pick_a = jnp.concatenate(pick_a, axis=0).astype(BF16)
    pick_b = jnp.concatenate(pick_b, axis=0).astype(BF16)
    order_col = lax.broadcasted_iota(jnp.int32, (pairs, 2 * pairs), 0)
    order_row = lax.broadcasted_iota(jnp.int32, (pairs, 2 * pairs), 1) % pairs
    owner_row = owner_row_ref[...]
    earlier = (owner_col_ref[...] == owner_row) & (order_col < order_row)
    slot = jnp.sum(jnp.where(earlier, 1, 0), axis=0, keepdims=True)
    side = lax.broadcasted_iota(jnp.int32, (1, 2 * pairs), 1) // pairs
    target = owner_row * 16 + side * 8 + slot
    place = jnp.where(lax.broadcasted_iota(jnp.int32, (16 * n, 2 * pairs), 0) == target, 1.0, 0.0).astype(BF16)

    copy_both.wait_recv()

    @pl.when(even)
    def _():
        even_other.start()

    odd_own.wait_recv()
    odd_other.wait_recv()

    step = 256

    def correlate(q, carry):
        lanes = pl.ds(pl.multiple_of(q * step, step), step)
        for h in range(2):
            a_v[h] = jnp.dot(pick_a, white[h, 0, :, lanes], preferred_element_type=F32).reshape(2, COMPS, pairs, step)
            b_v[h] = jnp.dot(
                pick_b, white[h, :, :, lanes].reshape(3 * group, step), preferred_element_type=F32
            ).reshape(2, COMPS, pairs, step)
        for i in range(5):
            kind = hour * 4 + i
            c, e = kind // COMPS, kind % COMPS
            re, im = 0.0, 0.0
            for h in range(2):
                ar, ai, br, bi = a_v[h, 0, c], a_v[h, 1, c], b_v[h, 0, e], b_v[h, 1, e]
                re = re + (ar * br + ai * bi)
                im = im + (ar * bi - ai * br)
            cross[pl.ds(i * pairs, pairs), lanes] = re.astype(BF16)
            cross[pl.ds(i * pairs, pairs), pl.ds(pl.multiple_of(NB + q * step, step), step)] = im.astype(BF16)
        return carry

    lax.fori_loop(0, NB // step, correlate, 0)
    for c in range(4):
        inv_copy(c).wait()

    def far_copy(part, source, dst):
        count = 5 - part
        return pltpu.make_async_remote_copy(
            src_ref=outgoing.at[dst, pl.ds(0, count), part], dst_ref=out_ref.at[source, pl.ds(0, count), part],
            send_sem=far_send.at[part, dst], recv_sem=far_recv.at[part, source],
            device_id=(dst, hour), device_id_type=MESH,
        )

    def own_copy(part):
        count = 5 - part
        return pltpu.make_async_copy(
            outgoing.at[me, pl.ds(0, count), part], out_ref.at[me, pl.ds(0, count), part], own_sem.at[part]
        )

    for part in range(2):
        count = 5 - part
        first_row = pl.multiple_of(part * hour * pairs, pairs)
        lag_half = hour if part == 0 else other
        source = cross[pl.ds(first_row, count * pairs), :]
        for side in range(2):
            lagged[side, pl.ds(0, count * pairs)] = jnp.dot(
                source, inv_v[lag_half * 2 + side], preferred_element_type=F32
            ).astype(BF16)
        for i in range(count):
            both = lagged[:, pl.ds(i * pairs, pairs)].reshape(2 * pairs, 256)
            moved = jnp.dot(place, both, preferred_element_type=F32).astype(BF16)
            outgoing[:, i, part] = moved.reshape(n, 16, 256)

        def send(step, carry, part=part):
            far_copy(part, me, lax.rem(me + step, n)).start()
            return carry

        lax.fori_loop(1, n, send, 0)
        own_copy(part).start()

    def finish(step, carry):
        peer = lax.rem(me + step, n)
        for part in range(2):
            copy = far_copy(part, peer, peer)
            copy.wait_send()
            copy.wait_recv()
        return carry

    lax.fori_loop(1, n, finish, 0)
    for part in range(2):
        own_copy(part).wait()
    copy_far.wait_send()
    copy_hour.wait_send()
    copy_both.wait_send()
    odd_own.wait_send()
    odd_other.wait_send()


def shards(windows, pair_first, pair_second, owners):
    n = lax.axis_size("sens")
    rows = windows.shape[1] * COMPS
    pairs = pair_first.shape[0]
    fwd, inv = (jnp.asarray(table) for table in folded_tables())
    vmem = pl.BlockSpec(memory_space=pltpu.VMEM)
    anywhere = pl.BlockSpec(memory_space=pl.ANY)
    received = pl.pallas_call(
        functools.partial(kernel, n, pairs),
        out_shape=jax.ShapeDtypeStruct((n, 5, 2, 16, 256), BF16),
        in_specs=[vmem] * 5 + [anywhere] * 2,
        out_specs=anywhere,
        scratch_shapes=[
            pltpu.VMEM(fwd.shape, BF16),
            pltpu.VMEM(inv.shape, BF16),
            pltpu.VMEM((8 * rows, HALF), BF16),
            pltpu.VMEM((2, rows, NB), F32),
            pltpu.VMEM((2, 3, 2 * rows, NB), BF16),
            pltpu.VMEM((2, 2, COMPS, pairs, 256), F32),
            pltpu.VMEM((2, 2, COMPS, pairs, 256), F32),
            pltpu.VMEM((5 * pairs, 2 * NB), BF16),
            pltpu.VMEM((2, 5 * pairs, 256), BF16),
            pltpu.VMEM((n, 5, 2, 16, 256), BF16),
            pltpu.SemaphoreType.DMA((CHUNKS,)),
            pltpu.SemaphoreType.DMA((4,)),
            pltpu.SemaphoreType.DMA((5,)),
            pltpu.SemaphoreType.DMA((5,)),
            pltpu.SemaphoreType.DMA((2, n)),
            pltpu.SemaphoreType.DMA((2, n)),
            pltpu.SemaphoreType.DMA((2,)),
        ],
        compiler_params=pltpu.CompilerParams(
            collective_id=0, has_side_effects=True, vmem_limit_bytes=50 * 2**20
        ),
    )(
        windows.reshape(rows, SAMPLES),
        pair_first[:, None],
        pair_second[:, None],
        owners,
        jnp.tile(owners[:, 0], 2)[None, :],
        fwd,
        inv,
    )
    received = received.reshape(n, 10, 2, 8, 256)[:, :9].transpose(0, 3, 1, 2, 4).reshape(n * 8, WIDTH // 2)
    return received.astype(F32) / jnp.sqrt(F32(2 * NB))


def solution(mesh):
    placed = (P("hour", "sens", None, None), P("sens"), P("sens"), P("sens", None))

    def run(windows, pair_first, pair_second, owners):
        n, hours = mesh.shape["sens"], mesh.shape["hour"]
        pairs = pair_first.shape[0] // n
        fits = hours == 2 and windows.shape[0] == 2 and n == 16 and pairs == 64 and windows.shape[1] == 8 * n
        body = shards if fits else plain_shards
        return jax.shard_map(
            body, mesh=mesh, in_specs=placed, out_specs=P("sens", "hour"), check_vma=False
        )(windows, pair_first, pair_second, owners)

    return run
```

```python
import functools

import jax
import jax.numpy as jnp
import ml_dtypes
import numpy as np
from jax import lax
from jax.experimental import pallas as pl
from jax.experimental.pallas import tpu as pltpu
from jax.sharding import PartitionSpec as P

SAMPLES = 4096
PADDED = 8192
NB = 2048
LAGS = 1024
COMPS = 3
WIDTH = COMPS * COMPS * LAGS
HALF = SAMPLES // 2
QUARTER = NB // 2
BLOCK = 128
CHUNKS = QUARTER // BLOCK
PIECES = 4
MESH = pl.DeviceIdType.MESH
F32 = jnp.float32
BF16 = jnp.bfloat16

def host_tables():
    times = np.arange(HALF, dtype=np.int64)
    bins = np.arange(NB, dtype=np.int64) + 1
    angle = (times[:, None] * bins[None, :] % PADDED) * (2.0 * np.pi / PADDED)
    fwd = np.concatenate([np.cos(angle), -np.sin(angle)], axis=1).astype(ml_dtypes.bfloat16)
    shifts = np.arange(LAGS, dtype=np.int64) - LAGS // 2
    back = (bins[:, None] * shifts[None, :] % PADDED) * (2.0 * np.pi / PADDED)
    inv = np.concatenate([np.cos(back), -np.sin(back)], axis=0).astype(ml_dtypes.bfloat16)
    return fwd, inv


def whiten(rows, fwd):
    count = rows.shape[0]
    both = jnp.concatenate([rows[:, :HALF], rows[:, HALF:]], axis=0)
    spec = jnp.dot(both, fwd, preferred_element_type=jnp.float32)
    ar, ai = spec[:count, :NB], spec[:count, NB:]
    br, bi = spec[count:, :NB], spec[count:, NB:]
    turn = (lax.broadcasted_iota(jnp.int32, (1, NB), 1) + 1) % 4
    even = turn % 2 == 0
    sign_re = jnp.where((turn == 0) | (turn == 1), 1.0, -1.0)
    sign_im = jnp.where((turn == 0) | (turn == 3), 1.0, -1.0)
    real_part = ar + sign_re * jnp.where(even, br, bi)
    imag_part = ai + sign_im * jnp.where(even, bi, br)
    power = real_part * real_part + imag_part * imag_part
    level = jnp.mean(power, axis=1, keepdims=True)
    scale = 1.0 / jnp.sqrt(power + 0.1 * level + 1e-06)
    return jnp.concatenate([real_part * scale, imag_part * scale], axis=1).astype(jnp.bfloat16)


def from_behind(value, axis, steps):
    count = lax.axis_size(axis)
    pairs = [(source, (source + steps) % count) for source in range(count)]
    return lax.ppermute(value, axis, pairs)


def pick(rows, index):
    table = (index[:, None] == jnp.arange(rows.shape[0], dtype=jnp.int32)[None, :]).astype(jnp.bfloat16)
    return jnp.dot(table, rows, preferred_element_type=jnp.float32)


def plain_shards(windows, pair_first, pair_second, owners):
    hours_here, sensors, _, _ = windows.shape
    pairs = pair_first.shape[0]
    hour_count = lax.axis_size("hour")
    owner_count = lax.axis_size("sens")
    hours = hours_here * hour_count
    columns = WIDTH // hour_count
    capacity = max(2, 2 * pairs // owner_count)
    fwd, inv = (jnp.asarray(table) for table in host_tables())

    white = whiten(windows.reshape(hours_here * sensors * COMPS, SAMPLES), fwd)
    white = lax.all_gather(white, "hour", axis=0, tiled=True)
    white = white.reshape(hours, sensors, COMPS * 2 * NB)
    nearer = from_behind(white, "sens", -1)
    farther = from_behind(white, "sens", -2)
    candidates = jnp.concatenate([white, nearer, farther], axis=1)

    start = lax.axis_index("hour") * columns
    first_block = start // LAGS
    blocks = min(COMPS * COMPS, max((h * columns + columns - 1) // LAGS - h * columns // LAGS + 1 for h in range(hour_count)))
    first_block = jnp.minimum(first_block, COMPS * COMPS - blocks)
    kinds = first_block + jnp.arange(blocks, dtype=jnp.int32)

    total_re, total_im = 0.0, 0.0
    for hour in range(hours):
        a = pick(white[hour], pair_first).reshape(pairs, COMPS, 2, NB)
        b = pick(candidates[hour], pair_second).reshape(pairs, COMPS, 2, NB)
        a = jnp.take(a, kinds // COMPS, axis=1)
        b = jnp.take(b, kinds % COMPS, axis=1)
        ar, ai, br, bi = a[:, :, 0], a[:, :, 1], b[:, :, 0], b[:, :, 1]
        total_re = total_re + (ar * br + ai * bi)
        total_im = total_im + (ar * bi - ai * br)
    cross = jnp.concatenate([total_re, total_im], axis=-1).astype(jnp.bfloat16)
    lagged = jnp.dot(cross.reshape(pairs * blocks, 2 * NB), inv, preferred_element_type=jnp.float32)
    lagged = lagged.astype(jnp.bfloat16).reshape(pairs, blocks * LAGS)
    lagged = lax.dynamic_slice_in_dim(lagged, start - first_block * LAGS, columns, axis=1)

    owner = owners[:, 0]
    order = jnp.arange(pairs, dtype=jnp.int32)
    earlier = (owner[:, None] == owner[None, :]) & (order[None, :] < order[:, None])
    target = owner * capacity + jnp.sum(earlier.astype(jnp.int32), axis=1)
    place = (jnp.arange(owner_count * capacity, dtype=jnp.int32)[:, None] == target[None, :]).astype(jnp.bfloat16)
    outgoing = jnp.dot(place, lagged, preferred_element_type=jnp.float32).astype(jnp.bfloat16)
    received = lax.all_to_all(outgoing, "sens", split_axis=0, concat_axis=0, tiled=True)
    return received.astype(jnp.float32) / jnp.sqrt(jnp.float32(NB * hours))


def folded_tables():
    times = np.arange(HALF, dtype=np.int64)
    bins = np.arange(QUARTER, dtype=np.int64)
    angle = (times[:, None] * bins[None, :] % PADDED) * (2.0 * np.pi / PADDED)
    cosine, sine = np.cos(angle), np.sin(angle)
    sine[:, 0] = 1 - 2 * (times // 4 % 2)
    both = np.stack([cosine.reshape(HALF, CHUNKS, BLOCK), sine.reshape(HALF, CHUNKS, BLOCK)], axis=2)
    fwd = both.transpose(1, 0, 2, 3).reshape(CHUNKS, HALF, 2 * BLOCK).astype(ml_dtypes.bfloat16)
    order = np.concatenate([bins, NB - bins])
    order[0] = QUARTER
    shifts = np.arange(LAGS, dtype=np.int64) - LAGS // 2
    back = (order[:, None] * shifts[None, :] % PADDED) * (2.0 * np.pi / PADDED)
    inv = np.concatenate([np.cos(back), -np.sin(back)], axis=0)
    inv = inv.reshape(2 * NB, 4, LAGS // 4).transpose(1, 0, 2).astype(ml_dtypes.bfloat16)
    return fwd, inv


def kernel(
    n, pairs, x_ref, first_ref, second_ref, owner_ref, fwd_hbm, inv_hbm, out_ref,
    fwd_v, inv_v, xm, spec, white, a_v, b_v, cross, lagged, outgoing,
    fwd_sem, inv_sem, near_send, near_recv, far_send, far_recv, own_sem,
):
    me = lax.axis_index("sens")
    hour = lax.axis_index("hour")
    other = 1 - hour

    barrier = pltpu.get_barrier_semaphore()

    def greet(step, carry):
        pl.semaphore_signal(barrier, inc=1, device_id=(lax.rem(me + step, n), hour), device_id_type=MESH)
        return carry

    lax.fori_loop(1, n, greet, 0)
    pl.semaphore_signal(barrier, inc=1, device_id=(me, other), device_id_type=MESH)

    def fwd_copy(c):
        return pltpu.make_async_copy(fwd_hbm.at[c], fwd_v.at[c], fwd_sem.at[c])

    def inv_copy(c):
        return pltpu.make_async_copy(inv_hbm.at[c], inv_v.at[c], inv_sem.at[c])

    for c in range(CHUNKS):
        fwd_copy(c).start()
    for c in range(4):
        inv_copy(c).start()

    rows = x_ref.shape[0]
    x = x_ref[...].astype(F32)
    halves = jnp.concatenate([x[:, :HALF], x[:, HALF:]], axis=0)
    residue = lax.broadcasted_iota(jnp.int32, (2 * rows, HALF), 1) & 3
    xm[...] = jnp.concatenate([jnp.where(residue == r, halves, 0.0) for r in range(4)], axis=0).astype(BF16)

    lane = lax.broadcasted_iota(jnp.int32, (rows, BLOCK), 1)
    turn = lane & 3
    root = 0.70703125

    def transform(c, total):
        fwd_copy(c).wait()
        part = jnp.dot(xm[...], fwd_v[c], preferred_element_type=F32)
        pc, ps = [], []
        for r in range(4):
            top = part[2 * r * rows:(2 * r + 1) * rows]
            low = part[(2 * r + 1) * rows:(2 * r + 2) * rows]
            c1, s1 = low[:, :BLOCK], low[:, BLOCK:]
            pc.append(top[:, :BLOCK] + jnp.where(turn == 0, c1, jnp.where(turn == 1, -s1, jnp.where(turn == 2, -c1, s1))))
            ps.append(top[:, BLOCK:] + jnp.where(turn == 0, s1, jnp.where(turn == 1, c1, jnp.where(turn == 2, -s1, -c1))))
        ends = (lane == 0) & (c == 0)
        re_a = jnp.where(ends, ps[0] + root * (ps[1] - ps[3]), pc[0] + pc[1] + pc[2] + pc[3])
        im_a = -jnp.where(ends, ps[2] + root * (ps[1] + ps[3]), ps[0] + ps[1] + ps[2] + ps[3])
        zero_sine = jnp.where(ends, 0.0, 1.0)
        re_b = pc[0] - pc[2] + zero_sine * (ps[1] - ps[3])
        im_b = pc[3] - pc[1] + zero_sine * (ps[0] - ps[2])
        near = pl.ds(pl.multiple_of(c * BLOCK, BLOCK), BLOCK)
        far = pl.ds(pl.multiple_of(QUARTER + c * BLOCK, BLOCK), BLOCK)
        spec[0, :, near] = re_a
        spec[0, :, far] = re_b
        spec[1, :, near] = im_a
        spec[1, :, far] = im_b
        return total + (re_a * re_a + im_a * im_a) + (re_b * re_b + im_b * im_b)

    total = lax.fori_loop(0, CHUNKS, transform, jnp.zeros((rows, BLOCK), F32))
    level = jnp.sum(total, axis=1, keepdims=True) * (1.0 / NB)
    real_part, imag_part = spec[0], spec[1]
    scale = 1.0 / jnp.sqrt(real_part * real_part + imag_part * imag_part + 0.1 * level + 1e-06)
    result = jnp.concatenate([real_part * scale, imag_part * scale], axis=0).astype(BF16)
    piece = NB // PIECES
    for p in range(PIECES):
        white[0, 0, p] = result[:, p * piece:(p + 1) * piece]

    pl.semaphore_wait(barrier, n)
    even = lax.rem(me, 2) == 0
    odd = lax.rem(me, 2) == 1
    behind = (lax.rem(me + n - 1, n), hour)
    behind2 = (lax.rem(me + n - 2, n), hour)
    ahead = (lax.rem(me + 1, n), hour)
    across = (me, other)

    def near_copy(p, src, dst, kind, device):
        return pltpu.make_async_remote_copy(
            src_ref=white.at[src[0], src[1], p], dst_ref=white.at[dst[0], dst[1], p],
            send_sem=near_send.at[kind, p], recv_sem=near_recv.at[kind, p], device_id=device, device_id_type=MESH,
        )

    def copy_far(p):
        return near_copy(p, (0, 0), (0, 2), 0, behind2)

    def copy_hour(p):
        return near_copy(p, (0, 0), (1, 0), 1, across)

    def copy_both(p):
        return near_copy(p, (0, 2), (1, 2), 2, across) if p % 2 == 0 else near_copy(p, (1, 0), (1, 2), 2, behind2)

    def odd_own(p):
        return near_copy(p, (0, 0), (0, 1), 3, behind)

    def even_own(p):
        return near_copy(p, (0, 2), (0, 1), 3, ahead)

    def odd_other(p):
        return near_copy(p, (1, 0), (1, 1), 4, behind)

    def even_other(p):
        return near_copy(p, (1, 2), (1, 1), 4, ahead)

    for p in range(PIECES):
        copy_far(p).start()
        copy_hour(p).start()

    @pl.when(odd)
    def _():
        for p in range(PIECES):
            odd_own(p).start()

    group = 2 * rows
    wide = lax.broadcasted_iota(jnp.int32, (pairs, 3 * group), 1)
    row_of = lax.broadcasted_iota(jnp.int32, (pairs, pairs), 0)
    column_of = lax.broadcasted_iota(jnp.int32, (pairs, pairs), 1)

    def upright(ref):
        return jnp.sum(jnp.where(row_of == column_of, ref[...], 0), axis=1, keepdims=True)

    first, second = upright(first_ref), upright(second_ref)
    second_base = second // 8 * group + second % 8
    pick_a, pick_b = [], []
    for part in range(2):
        for comp in range(2):
            shift = part * rows + (comp + hour) * 8
            pick_a.append(jnp.where(wide[:, :group] == first + shift, 1.0, 0.0))
        for comp in range(COMPS):
            pick_b.append(jnp.where(wide == second_base + (part * rows + comp * 8), 1.0, 0.0))
    pick_a = jnp.concatenate(pick_a, axis=0).astype(BF16)
    pick_b = jnp.concatenate(pick_b, axis=0).astype(BF16)
    owner_row = owner_ref[...]
    earlier = (upright(owner_ref) == owner_row) & (row_of < column_of)
    place_of = owner_row * 16 + jnp.sum(jnp.where(earlier, 1, 0), axis=0, keepdims=True)
    twice = lax.broadcasted_iota(jnp.int32, (pairs, 2 * pairs), 1) % pairs
    twice = jnp.where(twice == lax.broadcasted_iota(jnp.int32, (pairs, 2 * pairs), 0), 1.0, 0.0).astype(BF16)
    place_of = jnp.broadcast_to(place_of, (8, pairs)).astype(F32).astype(BF16)
    place_of = jnp.dot(place_of, twice, preferred_element_type=F32)[0:1]
    side = lax.broadcasted_iota(jnp.int32, (1, 2 * pairs), 1) // pairs
    target = place_of + (side * 8).astype(F32)
    spot = lax.broadcasted_iota(jnp.int32, (16 * n, 2 * pairs), 0).astype(F32)
    place = jnp.where(spot == target, 1.0, 0.0).astype(BF16)

    for p in range(PIECES):
        copy_far(p).wait_recv()
        if p % 2 == 0:
            copy_both(p).start()

        @pl.when(even)
        def _(p=p):
            even_own(p).start()

        copy_hour(p).wait_recv()
        if p % 2 == 1:
            copy_both(p).start()

        @pl.when(odd)
        def _(p=p):
            odd_other(p).start()

    step = 256

    def correlate(p):
        def body(q, carry):
            lanes = pl.ds(pl.multiple_of(q * step, step), step)
            for h in range(2):
                a_v[h] = jnp.dot(pick_a, white[h, 0, p, :, lanes], preferred_element_type=F32).reshape(2, 2, pairs, step)
                b_v[h] = jnp.dot(
                    pick_b, white[h, :, p, :, lanes].reshape(3 * group, step), preferred_element_type=F32
                ).reshape(2, COMPS, pairs, step)
            start = p * piece + q * step
            for i in range(5):
                kind = hour * 4 + i
                c, e = kind // COMPS - hour, kind % COMPS
                re, im = 0.0, 0.0
                for h in range(2):
                    ar, ai, br, bi = a_v[h, 0, c], a_v[h, 1, c], b_v[h, 0, e], b_v[h, 1, e]
                    re = re + (ar * br + ai * bi)
                    im = im + (ar * bi - ai * br)
                cross[pl.ds(i * pairs, pairs), pl.ds(pl.multiple_of(start, step), step)] = re.astype(BF16)
                cross[pl.ds(i * pairs, pairs), pl.ds(pl.multiple_of(NB + start, step), step)] = im.astype(BF16)
            return carry

        lax.fori_loop(0, piece // step, body, 0)

    def pass_on(p):
        copy_both(p).wait_recv()

        @pl.when(even)
        def _():
            even_other(p).start()

    pass_on(0)
    for p in range(PIECES):
        if p + 1 < PIECES:
            pass_on(p + 1)
        odd_own(p).wait_recv()
        odd_other(p).wait_recv()
        correlate(p)

    for c in range(4):
        inv_copy(c).wait()

    def far_copy(part, source, dst):
        count = 5 - part
        return pltpu.make_async_remote_copy(
            src_ref=outgoing.at[dst, pl.ds(0, count), part], dst_ref=out_ref.at[source, pl.ds(0, count), part],
            send_sem=far_send.at[part, dst], recv_sem=far_recv.at[part, source],
            device_id=(dst, hour), device_id_type=MESH,
        )

    def own_copy(part):
        count = 5 - part
        return pltpu.make_async_copy(
            outgoing.at[me, pl.ds(0, count), part], out_ref.at[me, pl.ds(0, count), part], own_sem.at[part]
        )

    for part in range(2):
        count = 5 - part
        first_row = pl.multiple_of(part * hour * pairs, pairs)
        lag_half = hour if part == 0 else other
        source = cross[pl.ds(first_row, count * pairs), :]
        for side in range(2):
            lagged[side, pl.ds(0, count * pairs)] = jnp.dot(
                source, inv_v[lag_half * 2 + side], preferred_element_type=F32
            ).astype(BF16)
        for i in range(count):
            both = lagged[:, pl.ds(i * pairs, pairs)].reshape(2 * pairs, 256)
            moved = jnp.dot(place, both, preferred_element_type=F32).astype(BF16)
            outgoing[:, i, part] = moved.reshape(n, 16, 256)

        home = me // 8 * 8

        def send(step, carry, part=part):
            far_copy(part, me, lax.rem(home + 8, n) + lax.rem(me + step, 8)).start()

            @pl.when(step > 0)
            def _():
                far_copy(part, me, home + lax.rem(me + step, 8)).start()

            return carry

        lax.fori_loop(0, 8, send, 0)
        own_copy(part).start()

    def finish(step, carry):
        peer = lax.rem(me + step, n)
        for part in range(2):
            copy = far_copy(part, peer, peer)
            copy.wait_send()
            copy.wait_recv()
        return carry

    lax.fori_loop(1, n, finish, 0)
    for part in range(2):
        own_copy(part).wait()
    for p in range(PIECES):
        for copy in (copy_far(p), copy_hour(p), copy_both(p), odd_own(p), odd_other(p)):
            copy.wait_send()


def shards(windows, pair_first, pair_second, owners):
    n = lax.axis_size("sens")
    rows = windows.shape[1] * COMPS
    pairs = pair_first.shape[0]
    fwd, inv = (jnp.asarray(table) for table in folded_tables())
    vmem = pl.BlockSpec(memory_space=pltpu.VMEM)
    anywhere = pl.BlockSpec(memory_space=pl.ANY)
    received = pl.pallas_call(
        functools.partial(kernel, n, pairs),
        out_shape=jax.ShapeDtypeStruct((n, 5, 2, 16, 256), BF16),
        in_specs=[vmem] * 4 + [anywhere] * 2,
        out_specs=anywhere,
        scratch_shapes=[
            pltpu.VMEM(fwd.shape, BF16),
            pltpu.VMEM(inv.shape, BF16),
            pltpu.VMEM((8 * rows, HALF), BF16),
            pltpu.VMEM((2, rows, NB), F32),
            pltpu.VMEM((2, 3, PIECES, 2 * rows, NB // PIECES), BF16),
            pltpu.VMEM((2, 2, 2, pairs, 256), F32),
            pltpu.VMEM((2, 2, COMPS, pairs, 256), F32),
            pltpu.VMEM((5 * pairs, 2 * NB), BF16),
            pltpu.VMEM((2, 5 * pairs, 256), BF16),
            pltpu.VMEM((n, 5, 2, 16, 256), BF16),
            pltpu.SemaphoreType.DMA((CHUNKS,)),
            pltpu.SemaphoreType.DMA((4,)),
            pltpu.SemaphoreType.DMA((5, PIECES)),
            pltpu.SemaphoreType.DMA((5, PIECES)),
            pltpu.SemaphoreType.DMA((2, n)),
            pltpu.SemaphoreType.DMA((2, n)),
            pltpu.SemaphoreType.DMA((2,)),
        ],
        compiler_params=pltpu.CompilerParams(
            collective_id=0, has_side_effects=True, vmem_limit_bytes=50 * 2**20
        ),
    )(
        windows[0].transpose(1, 0, 2).reshape(rows, SAMPLES),
        pair_first[None, :],
        pair_second[None, :],
        owners.reshape(1, pairs),
        fwd,
        inv,
    )
    received = received.reshape(n, 10, 2, 8, 256)[:, :9].transpose(0, 3, 1, 2, 4).reshape(n * 8, WIDTH // 2)
    return received.astype(F32) / jnp.sqrt(F32(2 * NB))


def solution(mesh):
    placed = (P("hour", "sens", None, None), P("sens"), P("sens"), P("sens", None))

    def run(windows, pair_first, pair_second, owners):
        n, hours = mesh.shape["sens"], mesh.shape["hour"]
        pairs = pair_first.shape[0] // n
        fits = hours == 2 and windows.shape[0] == 2 and n == 16 and pairs == 64 and windows.shape[1] == 8 * n
        body = shards if fits else plain_shards
        return jax.shard_map(
            body, mesh=mesh, in_specs=placed, out_specs=P("sens", "hour"), check_vma=False
        )(windows, pair_first, pair_second, owners)

    return run
```

```python
import functools

import jax
import jax.numpy as jnp
import ml_dtypes
import numpy as np
from jax import lax
from jax.experimental import pallas as pl
from jax.experimental.pallas import tpu as pltpu
from jax.sharding import PartitionSpec as P

SAMPLES = 4096
PADDED = 8192
NB = 2048
LAGS = 1024
COMPS = 3
WIDTH = COMPS * COMPS * LAGS
HALF = SAMPLES // 2
QUARTER = NB // 2
BLOCK = 128
CHUNKS = QUARTER // BLOCK
PIECES = 4
MESH = pl.DeviceIdType.MESH
F32 = jnp.float32
BF16 = jnp.bfloat16

def host_tables():
    times = np.arange(HALF, dtype=np.int64)
    bins = np.arange(NB, dtype=np.int64) + 1
    angle = (times[:, None] * bins[None, :] % PADDED) * (2.0 * np.pi / PADDED)
    fwd = np.concatenate([np.cos(angle), -np.sin(angle)], axis=1).astype(ml_dtypes.bfloat16)
    shifts = np.arange(LAGS, dtype=np.int64) - LAGS // 2
    back = (bins[:, None] * shifts[None, :] % PADDED) * (2.0 * np.pi / PADDED)
    inv = np.concatenate([np.cos(back), -np.sin(back)], axis=0).astype(ml_dtypes.bfloat16)
    return fwd, inv


def whiten(rows, fwd):
    count = rows.shape[0]
    both = jnp.concatenate([rows[:, :HALF], rows[:, HALF:]], axis=0)
    spec = jnp.dot(both, fwd, preferred_element_type=jnp.float32)
    ar, ai = spec[:count, :NB], spec[:count, NB:]
    br, bi = spec[count:, :NB], spec[count:, NB:]
    turn = (lax.broadcasted_iota(jnp.int32, (1, NB), 1) + 1) % 4
    even = turn % 2 == 0
    sign_re = jnp.where((turn == 0) | (turn == 1), 1.0, -1.0)
    sign_im = jnp.where((turn == 0) | (turn == 3), 1.0, -1.0)
    real_part = ar + sign_re * jnp.where(even, br, bi)
    imag_part = ai + sign_im * jnp.where(even, bi, br)
    power = real_part * real_part + imag_part * imag_part
    level = jnp.mean(power, axis=1, keepdims=True)
    scale = 1.0 / jnp.sqrt(power + 0.1 * level + 1e-06)
    return jnp.concatenate([real_part * scale, imag_part * scale], axis=1).astype(jnp.bfloat16)


def from_behind(value, axis, steps):
    count = lax.axis_size(axis)
    pairs = [(source, (source + steps) % count) for source in range(count)]
    return lax.ppermute(value, axis, pairs)


def pick(rows, index):
    table = (index[:, None] == jnp.arange(rows.shape[0], dtype=jnp.int32)[None, :]).astype(jnp.bfloat16)
    return jnp.dot(table, rows, preferred_element_type=jnp.float32)


def plain_shards(windows, pair_first, pair_second, owners):
    hours_here, sensors, _, _ = windows.shape
    pairs = pair_first.shape[0]
    hour_count = lax.axis_size("hour")
    owner_count = lax.axis_size("sens")
    hours = hours_here * hour_count
    columns = WIDTH // hour_count
    capacity = max(2, 2 * pairs // owner_count)
    fwd, inv = (jnp.asarray(table) for table in host_tables())

    white = whiten(windows.reshape(hours_here * sensors * COMPS, SAMPLES), fwd)
    white = lax.all_gather(white, "hour", axis=0, tiled=True)
    white = white.reshape(hours, sensors, COMPS * 2 * NB)
    nearer = from_behind(white, "sens", -1)
    farther = from_behind(white, "sens", -2)
    candidates = jnp.concatenate([white, nearer, farther], axis=1)

    start = lax.axis_index("hour") * columns
    first_block = start // LAGS
    blocks = min(COMPS * COMPS, max((h * columns + columns - 1) // LAGS - h * columns // LAGS + 1 for h in range(hour_count)))
    first_block = jnp.minimum(first_block, COMPS * COMPS - blocks)
    kinds = first_block + jnp.arange(blocks, dtype=jnp.int32)

    total_re, total_im = 0.0, 0.0
    for hour in range(hours):
        a = pick(white[hour], pair_first).reshape(pairs, COMPS, 2, NB)
        b = pick(candidates[hour], pair_second).reshape(pairs, COMPS, 2, NB)
        a = jnp.take(a, kinds // COMPS, axis=1)
        b = jnp.take(b, kinds % COMPS, axis=1)
        ar, ai, br, bi = a[:, :, 0], a[:, :, 1], b[:, :, 0], b[:, :, 1]
        total_re = total_re + (ar * br + ai * bi)
        total_im = total_im + (ar * bi - ai * br)
    cross = jnp.concatenate([total_re, total_im], axis=-1).astype(jnp.bfloat16)
    lagged = jnp.dot(cross.reshape(pairs * blocks, 2 * NB), inv, preferred_element_type=jnp.float32)
    lagged = lagged.astype(jnp.bfloat16).reshape(pairs, blocks * LAGS)
    lagged = lax.dynamic_slice_in_dim(lagged, start - first_block * LAGS, columns, axis=1)

    owner = owners[:, 0]
    order = jnp.arange(pairs, dtype=jnp.int32)
    earlier = (owner[:, None] == owner[None, :]) & (order[None, :] < order[:, None])
    target = owner * capacity + jnp.sum(earlier.astype(jnp.int32), axis=1)
    place = (jnp.arange(owner_count * capacity, dtype=jnp.int32)[:, None] == target[None, :]).astype(jnp.bfloat16)
    outgoing = jnp.dot(place, lagged, preferred_element_type=jnp.float32).astype(jnp.bfloat16)
    received = lax.all_to_all(outgoing, "sens", split_axis=0, concat_axis=0, tiled=True)
    return received.astype(jnp.float32) / jnp.sqrt(jnp.float32(NB * hours))


def folded_tables():
    times = np.arange(HALF, dtype=np.int64)
    bins = np.arange(QUARTER, dtype=np.int64)
    angle = (times[:, None] * bins[None, :] % PADDED) * (2.0 * np.pi / PADDED)
    cosine, sine = np.cos(angle), np.sin(angle)
    sine[:, 0] = 1 - 2 * (times // 4 % 2)
    both = np.stack([cosine.reshape(HALF, CHUNKS, BLOCK), sine.reshape(HALF, CHUNKS, BLOCK)], axis=2)
    fwd = both.transpose(1, 0, 2, 3).reshape(CHUNKS, HALF, 2 * BLOCK).astype(ml_dtypes.bfloat16)
    order = np.concatenate([bins, NB - bins])
    order[0] = QUARTER
    shifts = np.arange(LAGS, dtype=np.int64) - LAGS // 2
    back = (order[:, None] * shifts[None, :] % PADDED) * (2.0 * np.pi / PADDED)
    inv = np.concatenate([np.cos(back), -np.sin(back)], axis=0)
    inv = inv.reshape(2 * NB, 4, LAGS // 4).transpose(1, 0, 2).astype(ml_dtypes.bfloat16)
    return fwd, inv


def kernel(
    n, pairs, x_hbm, first_hbm, second_hbm, owner_hbm, fwd_hbm, inv_hbm, out_ref,
    x_ref, first_ref, second_ref, owner_ref, in_sem, fwd_v, inv_v, xm, spec, white, a_v, b_v, early, cross, lagged, outgoing,
    fwd_sem, inv_sem, near_send, near_recv, far_send, far_recv, own_sem,
):
    me = lax.axis_index("sens")
    hour = lax.axis_index("hour")
    other = 1 - hour

    inputs = [
        pltpu.make_async_copy(source, target, in_sem.at[k])
        for k, (source, target) in enumerate(
            ((x_hbm, x_ref), (first_hbm, first_ref), (second_hbm, second_ref), (owner_hbm, owner_ref))
        )
    ]

    def fwd_copy(c):
        return pltpu.make_async_copy(fwd_hbm.at[c], fwd_v.at[c], fwd_sem.at[c])

    def inv_copy(c):
        return pltpu.make_async_copy(inv_hbm.at[c], inv_v.at[c], inv_sem.at[c])

    for copy in inputs:
        copy.start()
    for c in range(CHUNKS):
        fwd_copy(c).start()
    for c in range(4):
        inv_copy(c).start()

    barrier = pltpu.get_barrier_semaphore()

    def greet(step, carry):
        pl.semaphore_signal(barrier, inc=1, device_id=(lax.rem(me + step, n), hour), device_id_type=MESH)
        return carry

    lax.fori_loop(1, n, greet, 0)
    pl.semaphore_signal(barrier, inc=1, device_id=(me, other), device_id_type=MESH)

    for copy in inputs:
        copy.wait()

    rows = x_ref.shape[0]
    x = x_ref[...].astype(F32)
    halves = jnp.concatenate([x[:, :HALF], x[:, HALF:]], axis=0)
    residue = lax.broadcasted_iota(jnp.int32, (2 * rows, HALF), 1) & 3
    xm[...] = jnp.concatenate([jnp.where(residue == r, halves, 0.0) for r in range(4)], axis=0).astype(BF16)

    lane = lax.broadcasted_iota(jnp.int32, (rows, BLOCK), 1)
    turn = lane & 3
    root = 0.70703125

    def transform(c, total):
        fwd_copy(c).wait()
        part = jnp.dot(xm[...], fwd_v[c], preferred_element_type=F32)
        pc, ps = [], []
        for r in range(4):
            top = part[2 * r * rows:(2 * r + 1) * rows]
            low = part[(2 * r + 1) * rows:(2 * r + 2) * rows]
            c1, s1 = low[:, :BLOCK], low[:, BLOCK:]
            pc.append(top[:, :BLOCK] + jnp.where(turn == 0, c1, jnp.where(turn == 1, -s1, jnp.where(turn == 2, -c1, s1))))
            ps.append(top[:, BLOCK:] + jnp.where(turn == 0, s1, jnp.where(turn == 1, c1, jnp.where(turn == 2, -s1, -c1))))
        ends = (lane == 0) & (c == 0)
        re_a = jnp.where(ends, ps[0] + root * (ps[1] - ps[3]), pc[0] + pc[1] + pc[2] + pc[3])
        im_a = -jnp.where(ends, ps[2] + root * (ps[1] + ps[3]), ps[0] + ps[1] + ps[2] + ps[3])
        zero_sine = jnp.where(ends, 0.0, 1.0)
        re_b = pc[0] - pc[2] + zero_sine * (ps[1] - ps[3])
        im_b = pc[3] - pc[1] + zero_sine * (ps[0] - ps[2])
        near = pl.ds(pl.multiple_of(c * BLOCK, BLOCK), BLOCK)
        far = pl.ds(pl.multiple_of(QUARTER + c * BLOCK, BLOCK), BLOCK)
        spec[0, :, near] = re_a
        spec[0, :, far] = re_b
        spec[1, :, near] = im_a
        spec[1, :, far] = im_b
        return total + (re_a * re_a + im_a * im_a) + (re_b * re_b + im_b * im_b)

    total = lax.fori_loop(0, CHUNKS, transform, jnp.zeros((rows, BLOCK), F32))
    level = jnp.sum(total, axis=1, keepdims=True) * (1.0 / NB)
    real_part, imag_part = spec[0], spec[1]
    scale = 1.0 / jnp.sqrt(real_part * real_part + imag_part * imag_part + 0.1 * level + 1e-06)
    result = jnp.concatenate([real_part * scale, imag_part * scale], axis=0).astype(BF16)
    piece = NB // PIECES
    for p in range(PIECES):
        white[0, 0, p] = result[:, p * piece:(p + 1) * piece]

    pl.semaphore_wait(barrier, n)
    even = lax.rem(me, 2) == 0
    odd = lax.rem(me, 2) == 1
    behind = (lax.rem(me + n - 1, n), hour)
    behind2 = (lax.rem(me + n - 2, n), hour)
    ahead = (lax.rem(me + 1, n), hour)
    across = (me, other)

    def near_copy(p, src, dst, kind, device):
        return pltpu.make_async_remote_copy(
            src_ref=white.at[src[0], src[1], p], dst_ref=white.at[dst[0], dst[1], p],
            send_sem=near_send.at[kind, p], recv_sem=near_recv.at[kind, p], device_id=device, device_id_type=MESH,
        )

    def copy_far(p):
        return near_copy(p, (0, 0), (0, 2), 0, behind2)

    def copy_hour(p):
        return near_copy(p, (0, 0), (1, 0), 1, across)

    def copy_both(p):
        return near_copy(p, (0, 2), (1, 2), 2, across) if p % 2 == 0 else near_copy(p, (1, 0), (1, 2), 2, behind2)

    def odd_own(p):
        return near_copy(p, (0, 0), (0, 1), 3, behind)

    def even_own(p):
        return near_copy(p, (0, 2), (0, 1), 3, ahead)

    def odd_other(p):
        return near_copy(p, (1, 0), (1, 1), 4, behind)

    def even_other(p):
        return near_copy(p, (1, 2), (1, 1), 4, ahead)

    for p in range(PIECES):
        copy_far(p).start()
        copy_hour(p).start()

    @pl.when(odd)
    def _():
        for p in range(PIECES):
            odd_own(p).start()

    group = 2 * rows
    wide = lax.broadcasted_iota(jnp.int32, (pairs, 3 * group), 1)
    row_of = lax.broadcasted_iota(jnp.int32, (pairs, pairs), 0)
    column_of = lax.broadcasted_iota(jnp.int32, (pairs, pairs), 1)

    def upright(ref):
        return jnp.sum(jnp.where(row_of == column_of, ref[...], 0), axis=1, keepdims=True)

    first, second = upright(first_ref), upright(second_ref)
    second_base = second // 8 * group + second % 8
    pick_a, pick_b = [], []
    for part in range(2):
        for comp in range(2):
            shift = part * rows + (comp + hour) * 8
            pick_a.append(jnp.where(wide[:, :group] == first + shift, 1.0, 0.0))
        for comp in range(COMPS):
            pick_b.append(jnp.where(wide == second_base + (part * rows + comp * 8), 1.0, 0.0))
    pick_a = jnp.concatenate(pick_a, axis=0).astype(BF16)
    pick_b = jnp.concatenate(pick_b, axis=0).astype(BF16)
    owner_row = owner_ref[...]
    earlier = (upright(owner_ref) == owner_row) & (row_of < column_of)
    place_of = owner_row * 16 + jnp.sum(jnp.where(earlier, 1, 0), axis=0, keepdims=True)
    twice = lax.broadcasted_iota(jnp.int32, (pairs, 2 * pairs), 1) % pairs
    twice = jnp.where(twice == lax.broadcasted_iota(jnp.int32, (pairs, 2 * pairs), 0), 1.0, 0.0).astype(BF16)
    place_of = jnp.broadcast_to(place_of, (8, pairs)).astype(F32).astype(BF16)
    place_of = jnp.dot(place_of, twice, preferred_element_type=F32)[0:1]
    side = lax.broadcasted_iota(jnp.int32, (1, 2 * pairs), 1) // pairs
    target = place_of + (side * 8).astype(F32)
    spot = lax.broadcasted_iota(jnp.int32, (16 * n, 2 * pairs), 0).astype(F32)
    place = jnp.where(spot == target, 1.0, 0.0).astype(BF16)

    step = 256

    def arrive(p):
        copy_far(p).wait_recv()
        if p % 2 == 0:
            copy_both(p).start()

        @pl.when(even)
        def _():
            even_own(p).start()

        copy_hour(p).wait_recv()
        if p % 2 == 1:
            copy_both(p).start()

        @pl.when(odd)
        def _():
            odd_other(p).start()

    def pass_on(p):
        copy_both(p).wait_recv()

        @pl.when(even)
        def _():
            even_other(p).start()

    def correlate(p, h):
        (odd_own, odd_other)[h](p).wait_recv()

        def body(q, carry):
            lanes = pl.ds(pl.multiple_of(q * step, step), step)
            a_v[...] = jnp.dot(pick_a, white[h, 0, p, :, lanes], preferred_element_type=F32).reshape(2, 2, pairs, step)
            b_v[...] = jnp.dot(
                pick_b, white[h, :, p, :, lanes].reshape(3 * group, step), preferred_element_type=F32
            ).reshape(2, COMPS, pairs, step)
            start = p * piece + q * step
            real_lanes = pl.ds(pl.multiple_of(start, step), step)
            imag_lanes = pl.ds(pl.multiple_of(NB + start, step), step)
            for i in range(5):
                kind = hour * 4 + i
                c, e = kind // COMPS - hour, kind % COMPS
                ar, ai, br, bi = a_v[0, c], a_v[1, c], b_v[0, e], b_v[1, e]
                re = ar * br + ai * bi
                im = ar * bi - ai * br
                here = pl.ds(i * pairs, pairs)
                if h == 0:
                    early[here, real_lanes] = re
                    early[here, imag_lanes] = im
                else:
                    cross[here, real_lanes] = (early[here, real_lanes] + re).astype(BF16)
                    cross[here, imag_lanes] = (early[here, imag_lanes] + im).astype(BF16)
            return carry

        lax.fori_loop(0, piece // step, body, 0)

    arrive(0)
    arrive(1)
    correlate(0, 0)
    arrive(2)
    correlate(1, 0)
    arrive(3)
    correlate(2, 0)
    pass_on(0)
    correlate(3, 0)
    pass_on(1)
    correlate(0, 1)
    pass_on(2)
    correlate(1, 1)
    pass_on(3)
    correlate(2, 1)
    correlate(3, 1)

    for c in range(4):
        inv_copy(c).wait()

    def far_copy(part, source, dst):
        count = 5 - part
        return pltpu.make_async_remote_copy(
            src_ref=outgoing.at[dst, pl.ds(0, count), part], dst_ref=out_ref.at[source, pl.ds(0, count), part],
            send_sem=far_send.at[part, dst], recv_sem=far_recv.at[part, source],
            device_id=(dst, hour), device_id_type=MESH,
        )

    def own_copy(part):
        count = 5 - part
        return pltpu.make_async_copy(
            outgoing.at[me, pl.ds(0, count), part], out_ref.at[me, pl.ds(0, count), part], own_sem.at[part]
        )

    for part in range(2):
        count = 5 - part
        first_row = pl.multiple_of(part * hour * pairs, pairs)
        lag_half = hour if part == 0 else other
        source = cross[pl.ds(first_row, count * pairs), :]
        for side in range(2):
            lagged[side, pl.ds(0, count * pairs)] = jnp.dot(
                source, inv_v[lag_half * 2 + side], preferred_element_type=F32
            ).astype(BF16)
        for i in range(count):
            both = lagged[:, pl.ds(i * pairs, pairs)].reshape(2 * pairs, 256)
            moved = jnp.dot(place, both, preferred_element_type=F32).astype(BF16)
            outgoing[:, i, part] = moved.reshape(n, 16, 256)

        home = me // 8 * 8

        def send(step, carry, part=part):
            far_copy(part, me, lax.rem(home + 8, n) + lax.rem(me + step, 8)).start()

            @pl.when(step > 0)
            def _():
                far_copy(part, me, home + lax.rem(me + step, 8)).start()

            return carry

        lax.fori_loop(0, 8, send, 0)
        own_copy(part).start()

    def finish(step, carry):
        peer = lax.rem(me + step, n)
        for part in range(2):
            copy = far_copy(part, peer, peer)
            copy.wait_send()
            copy.wait_recv()
        return carry

    lax.fori_loop(1, n, finish, 0)
    for part in range(2):
        own_copy(part).wait()
    for p in range(PIECES):
        for copy in (copy_far(p), copy_hour(p), copy_both(p), odd_own(p), odd_other(p)):
            copy.wait_send()


def shards(windows, pair_first, pair_second, owners):
    n = lax.axis_size("sens")
    rows = windows.shape[1] * COMPS
    pairs = pair_first.shape[0]
    fwd, inv = (jnp.asarray(table) for table in folded_tables())
    anywhere = pl.BlockSpec(memory_space=pl.ANY)
    received = pl.pallas_call(
        functools.partial(kernel, n, pairs),
        out_shape=jax.ShapeDtypeStruct((n, 5, 2, 16, 256), BF16),
        in_specs=[pl.BlockSpec(memory_space=pltpu.HBM)] * 6,
        out_specs=anywhere,
        scratch_shapes=[
            pltpu.VMEM((rows, SAMPLES), BF16),
            pltpu.VMEM((1, pairs), jnp.int32),
            pltpu.VMEM((1, pairs), jnp.int32),
            pltpu.VMEM((1, pairs), jnp.int32),
            pltpu.SemaphoreType.DMA((4,)),
            pltpu.VMEM(fwd.shape, BF16),
            pltpu.VMEM(inv.shape, BF16),
            pltpu.VMEM((8 * rows, HALF), BF16),
            pltpu.VMEM((2, rows, NB), F32),
            pltpu.VMEM((2, 3, PIECES, 2 * rows, NB // PIECES), BF16),
            pltpu.VMEM((2, 2, pairs, 256), F32),
            pltpu.VMEM((2, COMPS, pairs, 256), F32),
            pltpu.VMEM((5 * pairs, 2 * NB), F32),
            pltpu.VMEM((5 * pairs, 2 * NB), BF16),
            pltpu.VMEM((2, 5 * pairs, 256), BF16),
            pltpu.VMEM((n, 5, 2, 16, 256), BF16),
            pltpu.SemaphoreType.DMA((CHUNKS,)),
            pltpu.SemaphoreType.DMA((4,)),
            pltpu.SemaphoreType.DMA((5, PIECES)),
            pltpu.SemaphoreType.DMA((5, PIECES)),
            pltpu.SemaphoreType.DMA((2, n)),
            pltpu.SemaphoreType.DMA((2, n)),
            pltpu.SemaphoreType.DMA((2,)),
        ],
        compiler_params=pltpu.CompilerParams(
            collective_id=0, has_side_effects=True, vmem_limit_bytes=56 * 2**20
        ),
    )(
        windows[0].transpose(1, 0, 2).reshape(rows, SAMPLES),
        pair_first[None, :],
        pair_second[None, :],
        owners.reshape(1, pairs),
        fwd,
        inv,
    )
    received = received.reshape(n, 10, 2, 8, 256)[:, :9].transpose(0, 3, 1, 2, 4).reshape(n * 8, WIDTH // 2)
    return received.astype(F32) / jnp.sqrt(F32(2 * NB))


def solution(mesh):
    placed = (P("hour", "sens", None, None), P("sens"), P("sens"), P("sens", None))

    def run(windows, pair_first, pair_second, owners):
        n, hours = mesh.shape["sens"], mesh.shape["hour"]
        pairs = pair_first.shape[0] // n
        fits = hours == 2 and windows.shape[0] == 2 and n == 16 and pairs == 64 and windows.shape[1] == 8 * n
        body = shards if fits else plain_shards
        return jax.shard_map(
            body, mesh=mesh, in_specs=placed, out_specs=P("sens", "hour"), check_vma=False
        )(windows, pair_first, pair_second, owners)

    return run
```

```python
import functools

import jax
import jax.numpy as jnp
import ml_dtypes
import numpy as np
from jax import lax
from jax.experimental import pallas as pl
from jax.experimental.pallas import tpu as pltpu
from jax.sharding import PartitionSpec as P

SAMPLES = 4096
PADDED = 8192
NB = 2048
LAGS = 1024
COMPS = 3
WIDTH = COMPS * COMPS * LAGS
HALF = SAMPLES // 2
QUARTER = NB // 2
BLOCK = 128
CHUNKS = QUARTER // BLOCK
PIECES = 4
MESH = pl.DeviceIdType.MESH
F32 = jnp.float32
BF16 = jnp.bfloat16

def host_tables():
    times = np.arange(HALF, dtype=np.int64)
    bins = np.arange(NB, dtype=np.int64) + 1
    angle = (times[:, None] * bins[None, :] % PADDED) * (2.0 * np.pi / PADDED)
    fwd = np.concatenate([np.cos(angle), -np.sin(angle)], axis=1).astype(ml_dtypes.bfloat16)
    shifts = np.arange(LAGS, dtype=np.int64) - LAGS // 2
    back = (bins[:, None] * shifts[None, :] % PADDED) * (2.0 * np.pi / PADDED)
    inv = np.concatenate([np.cos(back), -np.sin(back)], axis=0).astype(ml_dtypes.bfloat16)
    return fwd, inv


def whiten(rows, fwd):
    count = rows.shape[0]
    both = jnp.concatenate([rows[:, :HALF], rows[:, HALF:]], axis=0)
    spec = jnp.dot(both, fwd, preferred_element_type=jnp.float32)
    ar, ai = spec[:count, :NB], spec[:count, NB:]
    br, bi = spec[count:, :NB], spec[count:, NB:]
    turn = (lax.broadcasted_iota(jnp.int32, (1, NB), 1) + 1) % 4
    even = turn % 2 == 0
    sign_re = jnp.where((turn == 0) | (turn == 1), 1.0, -1.0)
    sign_im = jnp.where((turn == 0) | (turn == 3), 1.0, -1.0)
    real_part = ar + sign_re * jnp.where(even, br, bi)
    imag_part = ai + sign_im * jnp.where(even, bi, br)
    power = real_part * real_part + imag_part * imag_part
    level = jnp.mean(power, axis=1, keepdims=True)
    scale = 1.0 / jnp.sqrt(power + 0.1 * level + 1e-06)
    return jnp.concatenate([real_part * scale, imag_part * scale], axis=1).astype(jnp.bfloat16)


def from_behind(value, axis, steps):
    count = lax.axis_size(axis)
    pairs = [(source, (source + steps) % count) for source in range(count)]
    return lax.ppermute(value, axis, pairs)


def pick(rows, index):
    table = (index[:, None] == jnp.arange(rows.shape[0], dtype=jnp.int32)[None, :]).astype(jnp.bfloat16)
    return jnp.dot(table, rows, preferred_element_type=jnp.float32)


def plain_shards(windows, pair_first, pair_second, owners):
    hours_here, sensors, _, _ = windows.shape
    pairs = pair_first.shape[0]
    hour_count = lax.axis_size("hour")
    owner_count = lax.axis_size("sens")
    hours = hours_here * hour_count
    columns = WIDTH // hour_count
    capacity = max(2, 2 * pairs // owner_count)
    fwd, inv = (jnp.asarray(table) for table in host_tables())

    white = whiten(windows.reshape(hours_here * sensors * COMPS, SAMPLES), fwd)
    white = lax.all_gather(white, "hour", axis=0, tiled=True)
    white = white.reshape(hours, sensors, COMPS * 2 * NB)
    nearer = from_behind(white, "sens", -1)
    farther = from_behind(white, "sens", -2)
    candidates = jnp.concatenate([white, nearer, farther], axis=1)

    start = lax.axis_index("hour") * columns
    first_block = start // LAGS
    blocks = min(COMPS * COMPS, max((h * columns + columns - 1) // LAGS - h * columns // LAGS + 1 for h in range(hour_count)))
    first_block = jnp.minimum(first_block, COMPS * COMPS - blocks)
    kinds = first_block + jnp.arange(blocks, dtype=jnp.int32)

    total_re, total_im = 0.0, 0.0
    for hour in range(hours):
        a = pick(white[hour], pair_first).reshape(pairs, COMPS, 2, NB)
        b = pick(candidates[hour], pair_second).reshape(pairs, COMPS, 2, NB)
        a = jnp.take(a, kinds // COMPS, axis=1)
        b = jnp.take(b, kinds % COMPS, axis=1)
        ar, ai, br, bi = a[:, :, 0], a[:, :, 1], b[:, :, 0], b[:, :, 1]
        total_re = total_re + (ar * br + ai * bi)
        total_im = total_im + (ar * bi - ai * br)
    cross = jnp.concatenate([total_re, total_im], axis=-1).astype(jnp.bfloat16)
    lagged = jnp.dot(cross.reshape(pairs * blocks, 2 * NB), inv, preferred_element_type=jnp.float32)
    lagged = lagged.astype(jnp.bfloat16).reshape(pairs, blocks * LAGS)
    lagged = lax.dynamic_slice_in_dim(lagged, start - first_block * LAGS, columns, axis=1)

    owner = owners[:, 0]
    order = jnp.arange(pairs, dtype=jnp.int32)
    earlier = (owner[:, None] == owner[None, :]) & (order[None, :] < order[:, None])
    target = owner * capacity + jnp.sum(earlier.astype(jnp.int32), axis=1)
    place = (jnp.arange(owner_count * capacity, dtype=jnp.int32)[:, None] == target[None, :]).astype(jnp.bfloat16)
    outgoing = jnp.dot(place, lagged, preferred_element_type=jnp.float32).astype(jnp.bfloat16)
    received = lax.all_to_all(outgoing, "sens", split_axis=0, concat_axis=0, tiled=True)
    return received.astype(jnp.float32) / jnp.sqrt(jnp.float32(NB * hours))


def folded_tables():
    times = np.arange(HALF, dtype=np.int64)
    bins = np.arange(QUARTER, dtype=np.int64)
    angle = (times[:, None] * bins[None, :] % PADDED) * (2.0 * np.pi / PADDED)
    cosine, sine = np.cos(angle), np.sin(angle)
    sine[:, 0] = 1 - 2 * (times // 4 % 2)
    both = np.stack([cosine.reshape(HALF, CHUNKS, BLOCK), sine.reshape(HALF, CHUNKS, BLOCK)], axis=2)
    fwd = both.transpose(1, 0, 2, 3).reshape(CHUNKS, HALF, 2 * BLOCK).astype(ml_dtypes.bfloat16)
    order = np.concatenate([bins, NB - bins])
    order[0] = QUARTER
    shifts = np.arange(LAGS, dtype=np.int64) - LAGS // 2
    back = (order[:, None] * shifts[None, :] % PADDED) * (2.0 * np.pi / PADDED)
    inv = np.concatenate([np.cos(back), -np.sin(back)], axis=0)
    inv = inv.reshape(2 * NB, 4, LAGS // 4).transpose(1, 0, 2).astype(ml_dtypes.bfloat16)
    return fwd, inv


def kernel(
    n, pairs, x_hbm, first_hbm, second_hbm, owner_hbm, fwd_hbm, inv_hbm, out_ref,
    x_ref, first_ref, second_ref, owner_ref, in_sem, fwd_v, inv_v, xm, spec, white, a_v, b_v, early, cross, lagged, outgoing,
    fwd_sem, inv_sem, near_send, near_recv, far_send, far_recv, own_sem,
):
    me = lax.axis_index("sens")
    hour = lax.axis_index("hour")
    other = 1 - hour

    inputs = [
        pltpu.make_async_copy(source, target, in_sem.at[k])
        for k, (source, target) in enumerate(
            ((x_hbm, x_ref), (first_hbm, first_ref), (second_hbm, second_ref), (owner_hbm, owner_ref))
        )
    ]

    def fwd_copy(c):
        return pltpu.make_async_copy(fwd_hbm.at[c], fwd_v.at[c], fwd_sem.at[c])

    def inv_copy(c):
        return pltpu.make_async_copy(inv_hbm.at[c], inv_v.at[c], inv_sem.at[c])

    for copy in inputs:
        copy.start()
    for c in range(CHUNKS):
        fwd_copy(c).start()

    barrier = pltpu.get_barrier_semaphore()

    def greet(step, carry):
        pl.semaphore_signal(barrier, inc=1, device_id=(lax.rem(me + step, n), hour), device_id_type=MESH)
        return carry

    lax.fori_loop(1, n, greet, 0)
    pl.semaphore_signal(barrier, inc=1, device_id=(me, other), device_id_type=MESH)

    for copy in inputs:
        copy.wait()

    rows = x_ref.shape[0]
    x = x_ref[...].astype(F32)
    halves = jnp.concatenate([x[:, :HALF], x[:, HALF:]], axis=0)
    residue = lax.broadcasted_iota(jnp.int32, (2 * rows, HALF), 1) & 3
    xm[...] = jnp.concatenate([jnp.where(residue == r, halves, 0.0) for r in range(4)], axis=0).astype(BF16)

    lane = lax.broadcasted_iota(jnp.int32, (rows, BLOCK), 1)
    turn = lane & 3
    root = 0.70703125

    def transform(c, total):
        fwd_copy(c).wait()
        part = jnp.dot(xm[...], fwd_v[c], preferred_element_type=F32)
        pc, ps = [], []
        for r in range(4):
            top = part[2 * r * rows:(2 * r + 1) * rows]
            low = part[(2 * r + 1) * rows:(2 * r + 2) * rows]
            c1, s1 = low[:, :BLOCK], low[:, BLOCK:]
            pc.append(top[:, :BLOCK] + jnp.where(turn == 0, c1, jnp.where(turn == 1, -s1, jnp.where(turn == 2, -c1, s1))))
            ps.append(top[:, BLOCK:] + jnp.where(turn == 0, s1, jnp.where(turn == 1, c1, jnp.where(turn == 2, -s1, -c1))))
        ends = (lane == 0) & (c == 0)
        re_a = jnp.where(ends, ps[0] + root * (ps[1] - ps[3]), pc[0] + pc[1] + pc[2] + pc[3])
        im_a = -jnp.where(ends, ps[2] + root * (ps[1] + ps[3]), ps[0] + ps[1] + ps[2] + ps[3])
        zero_sine = jnp.where(ends, 0.0, 1.0)
        re_b = pc[0] - pc[2] + zero_sine * (ps[1] - ps[3])
        im_b = pc[3] - pc[1] + zero_sine * (ps[0] - ps[2])
        near = pl.ds(pl.multiple_of(c * BLOCK, BLOCK), BLOCK)
        far = pl.ds(pl.multiple_of(QUARTER + c * BLOCK, BLOCK), BLOCK)
        spec[0, :, near] = re_a
        spec[0, :, far] = re_b
        spec[1, :, near] = im_a
        spec[1, :, far] = im_b
        return total + (re_a * re_a + im_a * im_a) + (re_b * re_b + im_b * im_b)

    total = lax.fori_loop(0, CHUNKS, transform, jnp.zeros((rows, BLOCK), F32))
    for c in range(4):
        inv_copy(c).start()
    level = jnp.sum(total, axis=1, keepdims=True) * (1.0 / NB)
    real_part, imag_part = spec[0], spec[1]
    scale = 1.0 / jnp.sqrt(real_part * real_part + imag_part * imag_part + 0.1 * level + 1e-06)
    result = jnp.concatenate([real_part * scale, imag_part * scale], axis=0).astype(BF16)
    piece = NB // PIECES
    for p in range(PIECES):
        white[0, 0, p] = result[:, p * piece:(p + 1) * piece]

    pl.semaphore_wait(barrier, n)
    even = lax.rem(me, 2) == 0
    odd = lax.rem(me, 2) == 1
    behind = (lax.rem(me + n - 1, n), hour)
    behind2 = (lax.rem(me + n - 2, n), hour)
    ahead = (lax.rem(me + 1, n), hour)
    across = (me, other)

    def near_copy(p, src, dst, kind, device):
        return pltpu.make_async_remote_copy(
            src_ref=white.at[src[0], src[1], p], dst_ref=white.at[dst[0], dst[1], p],
            send_sem=near_send.at[kind, p], recv_sem=near_recv.at[kind, p], device_id=device, device_id_type=MESH,
        )

    def copy_far(p):
        return near_copy(p, (0, 0), (0, 2), 0, behind2)

    def copy_hour(p):
        return near_copy(p, (0, 0), (1, 0), 1, across)

    def copy_both(p):
        return near_copy(p, (0, 2), (1, 2), 2, across) if p % 2 == 0 else near_copy(p, (1, 0), (1, 2), 2, behind2)

    def odd_own(p):
        return near_copy(p, (0, 0), (0, 1), 3, behind)

    def even_own(p):
        return near_copy(p, (0, 2), (0, 1), 3, ahead)

    def odd_other(p):
        return near_copy(p, (1, 0), (1, 1), 4, behind)

    def even_other(p):
        return near_copy(p, (1, 2), (1, 1), 4, ahead)

    for p in range(PIECES):
        copy_far(p).start()
        copy_hour(p).start()

    @pl.when(odd)
    def _():
        for p in range(PIECES):
            odd_own(p).start()

    group = 2 * rows
    wide = lax.broadcasted_iota(jnp.int32, (pairs, 3 * group), 1)
    row_of = lax.broadcasted_iota(jnp.int32, (pairs, pairs), 0)
    column_of = lax.broadcasted_iota(jnp.int32, (pairs, pairs), 1)

    def upright(ref):
        return jnp.sum(jnp.where(row_of == column_of, ref[...], 0), axis=1, keepdims=True)

    first, second = upright(first_ref), upright(second_ref)
    second_base = second // 8 * group + second % 8
    pick_a, pick_b = [], []
    for part in range(2):
        for comp in range(2):
            shift = part * rows + (comp + hour) * 8
            pick_a.append(jnp.where(wide[:, :group] == first + shift, 1.0, 0.0))
        for comp in range(COMPS):
            pick_b.append(jnp.where(wide == second_base + (part * rows + comp * 8), 1.0, 0.0))
    pick_a = jnp.concatenate(pick_a, axis=0).astype(BF16)
    pick_b = jnp.concatenate(pick_b, axis=0).astype(BF16)
    owner_row = owner_ref[...]
    earlier = (upright(owner_ref) == owner_row) & (row_of < column_of)
    place_of = owner_row * 16 + jnp.sum(jnp.where(earlier, 1, 0), axis=0, keepdims=True)
    twice = lax.broadcasted_iota(jnp.int32, (pairs, 2 * pairs), 1) % pairs
    twice = jnp.where(twice == lax.broadcasted_iota(jnp.int32, (pairs, 2 * pairs), 0), 1.0, 0.0).astype(BF16)
    place_of = jnp.broadcast_to(place_of, (8, pairs)).astype(F32).astype(BF16)
    place_of = jnp.dot(place_of, twice, preferred_element_type=F32)[0:1]
    side = lax.broadcasted_iota(jnp.int32, (1, 2 * pairs), 1) // pairs
    target = place_of + (side * 8).astype(F32)
    spot = lax.broadcasted_iota(jnp.int32, (16 * n, 2 * pairs), 0).astype(F32)
    place = jnp.where(spot == target, 1.0, 0.0).astype(BF16)

    step = 256

    def arrive(p):
        copy_far(p).wait_recv()
        if p % 2 == 0:
            copy_both(p).start()

        @pl.when(even)
        def _():
            even_own(p).start()

        copy_hour(p).wait_recv()
        if p % 2 == 1:
            copy_both(p).start()

        @pl.when(odd)
        def _():
            odd_other(p).start()

    def pass_on(p):
        copy_both(p).wait_recv()

        @pl.when(even)
        def _():
            even_other(p).start()

    def correlate(p, h):
        (odd_own, odd_other)[h](p).wait_recv()

        def body(q, carry):
            lanes = pl.ds(pl.multiple_of(q * step, step), step)
            a_v[...] = jnp.dot(pick_a, white[h, 0, p, :, lanes], preferred_element_type=F32).reshape(2, 2, pairs, step)
            b_v[...] = jnp.dot(
                pick_b, white[h, :, p, :, lanes].reshape(3 * group, step), preferred_element_type=F32
            ).reshape(2, COMPS, pairs, step)
            start = p * piece + q * step
            real_lanes = pl.ds(pl.multiple_of(start, step), step)
            imag_lanes = pl.ds(pl.multiple_of(NB + start, step), step)
            for i in range(5):
                kind = hour * 4 + i
                c, e = kind // COMPS - hour, kind % COMPS
                ar, ai, br, bi = a_v[0, c], a_v[1, c], b_v[0, e], b_v[1, e]
                re = ar * br + ai * bi
                im = ar * bi - ai * br
                here = pl.ds(i * pairs, pairs)
                if h == 0:
                    early[here, real_lanes] = re
                    early[here, imag_lanes] = im
                else:
                    cross[here, real_lanes] = (early[here, real_lanes] + re).astype(BF16)
                    cross[here, imag_lanes] = (early[here, imag_lanes] + im).astype(BF16)
            return carry

        lax.fori_loop(0, piece // step, body, 0)

    arrive(0)
    arrive(1)
    correlate(0, 0)
    arrive(2)
    correlate(1, 0)
    arrive(3)
    correlate(2, 0)
    pass_on(0)
    correlate(3, 0)
    pass_on(1)
    correlate(0, 1)
    pass_on(2)
    correlate(1, 1)
    pass_on(3)
    correlate(2, 1)
    correlate(3, 1)

    for c in range(4):
        inv_copy(c).wait()

    spans = (pl.ds(0, 5), pl.ds(5, 4))

    def far_copy(part, source, dst):
        return pltpu.make_async_remote_copy(
            src_ref=outgoing.at[dst, spans[part]], dst_ref=out_ref.at[source, spans[part]],
            send_sem=far_send.at[part, dst], recv_sem=far_recv.at[part, source],
            device_id=(dst, hour), device_id_type=MESH,
        )

    def own_copy(part):
        return pltpu.make_async_copy(outgoing.at[me, spans[part]], out_ref.at[me, spans[part]], own_sem.at[part])

    for part in range(2):
        for lag_half, units, skip in ((hour, ((0, 2, 4), (6, 8))[part], 0), (other, ((1, 3), (5, 7))[part], hour)):
            count = len(units)
            first_row = pl.multiple_of((units[0] // 2 + skip) * pairs, pairs)
            source = cross[pl.ds(first_row, count * pairs), :]
            for side in range(2):
                lagged[side, pl.ds(0, count * pairs)] = jnp.dot(
                    source, inv_v[lag_half * 2 + side], preferred_element_type=F32
                ).astype(BF16)
            for i, unit in enumerate(units):
                both = lagged[:, pl.ds(i * pairs, pairs)].reshape(2 * pairs, 256)
                moved = jnp.dot(place, both, preferred_element_type=F32).astype(BF16)
                outgoing[:, unit] = moved.reshape(n, 16, 256)

        home = me // 8 * 8

        def send(step, carry, part=part):
            far_copy(part, me, lax.rem(home + 8, n) + lax.rem(me + step, 8)).start()

            @pl.when(step > 0)
            def _():
                far_copy(part, me, home + lax.rem(me + step, 8)).start()

            return carry

        lax.fori_loop(0, 8, send, 0)
        own_copy(part).start()

    def finish(step, carry):
        peer = lax.rem(me + step, n)
        for part in range(2):
            copy = far_copy(part, peer, peer)
            copy.wait_send()
            copy.wait_recv()
        return carry

    lax.fori_loop(1, n, finish, 0)
    for part in range(2):
        own_copy(part).wait()
    for p in range(PIECES):
        for copy in (copy_far(p), copy_hour(p), copy_both(p), odd_own(p), odd_other(p)):
            copy.wait_send()


def shards(windows, pair_first, pair_second, owners):
    n = lax.axis_size("sens")
    rows = windows.shape[1] * COMPS
    pairs = pair_first.shape[0]
    fwd, inv = (jnp.asarray(table) for table in folded_tables())
    received = pl.pallas_call(
        functools.partial(kernel, n, pairs),
        out_shape=jax.ShapeDtypeStruct((n, 9, 16, 256), BF16),
        in_specs=[pl.BlockSpec(memory_space=pltpu.HBM)] * 6,
        out_specs=pl.BlockSpec(memory_space=pltpu.VMEM),
        scratch_shapes=[
            pltpu.VMEM((rows, SAMPLES), BF16),
            pltpu.VMEM((1, pairs), jnp.int32),
            pltpu.VMEM((1, pairs), jnp.int32),
            pltpu.VMEM((1, pairs), jnp.int32),
            pltpu.SemaphoreType.DMA((4,)),
            pltpu.VMEM(fwd.shape, BF16),
            pltpu.VMEM(inv.shape, BF16),
            pltpu.VMEM((8 * rows, HALF), BF16),
            pltpu.VMEM((2, rows, NB), F32),
            pltpu.VMEM((2, 3, PIECES, 2 * rows, NB // PIECES), BF16),
            pltpu.VMEM((2, 2, pairs, 256), F32),
            pltpu.VMEM((2, COMPS, pairs, 256), F32),
            pltpu.VMEM((5 * pairs, 2 * NB), F32),
            pltpu.VMEM((5 * pairs, 2 * NB), BF16),
            pltpu.VMEM((2, 3 * pairs, 256), BF16),
            pltpu.VMEM((n, 9, 16, 256), BF16),
            pltpu.SemaphoreType.DMA((CHUNKS,)),
            pltpu.SemaphoreType.DMA((4,)),
            pltpu.SemaphoreType.DMA((5, PIECES)),
            pltpu.SemaphoreType.DMA((5, PIECES)),
            pltpu.SemaphoreType.DMA((2, n)),
            pltpu.SemaphoreType.DMA((2, n)),
            pltpu.SemaphoreType.DMA((2,)),
        ],
        compiler_params=pltpu.CompilerParams(
            collective_id=0, has_side_effects=True, vmem_limit_bytes=44 * 2**20
        ),
    )(
        windows[0].transpose(1, 0, 2).reshape(rows, SAMPLES),
        pair_first[None, :],
        pair_second[None, :],
        owners.reshape(1, pairs),
        fwd,
        inv,
    )
    received = received.reshape(n, 9, 2, 8, 256).transpose(0, 3, 1, 2, 4).reshape(n * 8, WIDTH // 2)
    return received.astype(F32) / jnp.sqrt(F32(2 * NB))


def solution(mesh):
    placed = (P("hour", "sens", None, None), P("sens"), P("sens"), P("sens", None))

    def run(windows, pair_first, pair_second, owners):
        n, hours = mesh.shape["sens"], mesh.shape["hour"]
        pairs = pair_first.shape[0] // n
        fits = hours == 2 and windows.shape[0] == 2 and n == 16 and pairs == 64 and windows.shape[1] == 8 * n
        body = shards if fits else plain_shards
        return jax.shard_map(
            body, mesh=mesh, in_specs=placed, out_specs=P("sens", "hour"), check_vma=False
        )(windows, pair_first, pair_second, owners)

    return run
```

```python
import functools

import jax
import jax.numpy as jnp
import ml_dtypes
import numpy as np
from jax import lax
from jax.experimental import pallas as pl
from jax.experimental.pallas import tpu as pltpu
from jax.sharding import PartitionSpec as P

SAMPLES = 4096
PADDED = 8192
NB = 2048
LAGS = 1024
COMPS = 3
WIDTH = COMPS * COMPS * LAGS
HALF = SAMPLES // 2
QUARTER = NB // 2
BLOCK = 128
CHUNKS = QUARTER // BLOCK
PIECES = 4
MESH = pl.DeviceIdType.MESH
F32 = jnp.float32
BF16 = jnp.bfloat16

def host_tables():
    times = np.arange(HALF, dtype=np.int64)
    bins = np.arange(NB, dtype=np.int64) + 1
    angle = (times[:, None] * bins[None, :] % PADDED) * (2.0 * np.pi / PADDED)
    fwd = np.concatenate([np.cos(angle), -np.sin(angle)], axis=1).astype(ml_dtypes.bfloat16)
    shifts = np.arange(LAGS, dtype=np.int64) - LAGS // 2
    back = (bins[:, None] * shifts[None, :] % PADDED) * (2.0 * np.pi / PADDED)
    inv = np.concatenate([np.cos(back), -np.sin(back)], axis=0).astype(ml_dtypes.bfloat16)
    return fwd, inv


def whiten(rows, fwd):
    count = rows.shape[0]
    both = jnp.concatenate([rows[:, :HALF], rows[:, HALF:]], axis=0)
    spec = jnp.dot(both, fwd, preferred_element_type=jnp.float32)
    ar, ai = spec[:count, :NB], spec[:count, NB:]
    br, bi = spec[count:, :NB], spec[count:, NB:]
    turn = (lax.broadcasted_iota(jnp.int32, (1, NB), 1) + 1) % 4
    even = turn % 2 == 0
    sign_re = jnp.where((turn == 0) | (turn == 1), 1.0, -1.0)
    sign_im = jnp.where((turn == 0) | (turn == 3), 1.0, -1.0)
    real_part = ar + sign_re * jnp.where(even, br, bi)
    imag_part = ai + sign_im * jnp.where(even, bi, br)
    power = real_part * real_part + imag_part * imag_part
    level = jnp.mean(power, axis=1, keepdims=True)
    scale = 1.0 / jnp.sqrt(power + 0.1 * level + 1e-06)
    return jnp.concatenate([real_part * scale, imag_part * scale], axis=1).astype(jnp.bfloat16)


def from_behind(value, axis, steps):
    count = lax.axis_size(axis)
    pairs = [(source, (source + steps) % count) for source in range(count)]
    return lax.ppermute(value, axis, pairs)


def pick(rows, index):
    table = (index[:, None] == jnp.arange(rows.shape[0], dtype=jnp.int32)[None, :]).astype(jnp.bfloat16)
    return jnp.dot(table, rows, preferred_element_type=jnp.float32)


def plain_shards(windows, pair_first, pair_second, owners):
    hours_here, sensors, _, _ = windows.shape
    pairs = pair_first.shape[0]
    hour_count = lax.axis_size("hour")
    owner_count = lax.axis_size("sens")
    hours = hours_here * hour_count
    columns = WIDTH // hour_count
    capacity = max(2, 2 * pairs // owner_count)
    fwd, inv = (jnp.asarray(table) for table in host_tables())

    white = whiten(windows.reshape(hours_here * sensors * COMPS, SAMPLES), fwd)
    white = lax.all_gather(white, "hour", axis=0, tiled=True)
    white = white.reshape(hours, sensors, COMPS * 2 * NB)
    nearer = from_behind(white, "sens", -1)
    farther = from_behind(white, "sens", -2)
    candidates = jnp.concatenate([white, nearer, farther], axis=1)

    start = lax.axis_index("hour") * columns
    first_block = start // LAGS
    blocks = min(COMPS * COMPS, max((h * columns + columns - 1) // LAGS - h * columns // LAGS + 1 for h in range(hour_count)))
    first_block = jnp.minimum(first_block, COMPS * COMPS - blocks)
    kinds = first_block + jnp.arange(blocks, dtype=jnp.int32)

    total_re, total_im = 0.0, 0.0
    for hour in range(hours):
        a = pick(white[hour], pair_first).reshape(pairs, COMPS, 2, NB)
        b = pick(candidates[hour], pair_second).reshape(pairs, COMPS, 2, NB)
        a = jnp.take(a, kinds // COMPS, axis=1)
        b = jnp.take(b, kinds % COMPS, axis=1)
        ar, ai, br, bi = a[:, :, 0], a[:, :, 1], b[:, :, 0], b[:, :, 1]
        total_re = total_re + (ar * br + ai * bi)
        total_im = total_im + (ar * bi - ai * br)
    cross = jnp.concatenate([total_re, total_im], axis=-1).astype(jnp.bfloat16)
    lagged = jnp.dot(cross.reshape(pairs * blocks, 2 * NB), inv, preferred_element_type=jnp.float32)
    lagged = lagged.astype(jnp.bfloat16).reshape(pairs, blocks * LAGS)
    lagged = lax.dynamic_slice_in_dim(lagged, start - first_block * LAGS, columns, axis=1)

    owner = owners[:, 0]
    order = jnp.arange(pairs, dtype=jnp.int32)
    earlier = (owner[:, None] == owner[None, :]) & (order[None, :] < order[:, None])
    target = owner * capacity + jnp.sum(earlier.astype(jnp.int32), axis=1)
    place = (jnp.arange(owner_count * capacity, dtype=jnp.int32)[:, None] == target[None, :]).astype(jnp.bfloat16)
    outgoing = jnp.dot(place, lagged, preferred_element_type=jnp.float32).astype(jnp.bfloat16)
    received = lax.all_to_all(outgoing, "sens", split_axis=0, concat_axis=0, tiled=True)
    return received.astype(jnp.float32) / jnp.sqrt(jnp.float32(NB * hours))


def folded_tables():
    times = np.arange(HALF, dtype=np.int64)
    bins = np.arange(QUARTER, dtype=np.int64)
    angle = (times[:, None] * bins[None, :] % PADDED) * (2.0 * np.pi / PADDED)
    cosine, sine = np.cos(angle), np.sin(angle)
    sine[:, 0] = 1 - 2 * (times // 4 % 2)
    both = np.stack([cosine.reshape(HALF, CHUNKS, BLOCK), sine.reshape(HALF, CHUNKS, BLOCK)], axis=2)
    fwd = both.transpose(1, 0, 2, 3).reshape(CHUNKS, HALF, 2 * BLOCK).astype(ml_dtypes.bfloat16)
    order = np.concatenate([bins, NB - bins])
    order[0] = QUARTER
    shifts = np.arange(LAGS, dtype=np.int64) - LAGS // 2
    back = (order[:, None] * shifts[None, :] % PADDED) * (2.0 * np.pi / PADDED)
    inv = np.concatenate([np.cos(back), -np.sin(back)], axis=0)
    inv = inv.reshape(2 * NB, 4, LAGS // 4).transpose(1, 0, 2).astype(ml_dtypes.bfloat16)
    return fwd, inv


def kernel(
    n, pairs, x_hbm, first_hbm, second_hbm, owner_hbm, fwd_hbm, inv_hbm, out_ref,
    x_ref, first_ref, second_ref, owner_ref, in_sem, fwd_v, inv_v, xm, spec, white, a_v, b_v, early, cross, lagged, outgoing,
    fwd_sem, inv_sem, near_send, near_recv, far_send, far_recv, own_sem,
):
    me = lax.axis_index("sens")
    hour = lax.axis_index("hour")
    other = 1 - hour

    inputs = [
        pltpu.make_async_copy(source, target, in_sem.at[k])
        for k, (source, target) in enumerate(
            ((x_hbm, x_ref), (first_hbm, first_ref), (second_hbm, second_ref), (owner_hbm, owner_ref))
        )
    ]

    def fwd_copy(c):
        return pltpu.make_async_copy(fwd_hbm.at[c], fwd_v.at[c], fwd_sem.at[c])

    def inv_copy(c):
        return pltpu.make_async_copy(inv_hbm.at[c], inv_v.at[c], inv_sem.at[c])

    for copy in inputs:
        copy.start()
    for c in range(CHUNKS):
        fwd_copy(c).start()

    barrier = pltpu.get_barrier_semaphore()

    def greet(step, carry):
        pl.semaphore_signal(barrier, inc=1, device_id=(lax.rem(me + step, n), hour), device_id_type=MESH)
        return carry

    lax.fori_loop(1, n, greet, 0)
    pl.semaphore_signal(barrier, inc=1, device_id=(me, other), device_id_type=MESH)

    for copy in inputs:
        copy.wait()

    rows = x_ref.shape[0]
    x = x_ref[...].astype(F32)
    halves = jnp.concatenate([x[:, :HALF], x[:, HALF:]], axis=0)
    residue = lax.broadcasted_iota(jnp.int32, (2 * rows, HALF), 1) & 3
    xm[...] = jnp.concatenate([jnp.where(residue == r, halves, 0.0) for r in range(4)], axis=0).astype(BF16)

    lane = lax.broadcasted_iota(jnp.int32, (rows, BLOCK), 1)
    turn = lane & 3
    root = 0.70703125

    def transform(c, total):
        fwd_copy(c).wait()
        part = jnp.dot(xm[...], fwd_v[c], preferred_element_type=F32)
        pc, ps = [], []
        for r in range(4):
            top = part[2 * r * rows:(2 * r + 1) * rows]
            low = part[(2 * r + 1) * rows:(2 * r + 2) * rows]
            c1, s1 = low[:, :BLOCK], low[:, BLOCK:]
            pc.append(top[:, :BLOCK] + jnp.where(turn == 0, c1, jnp.where(turn == 1, -s1, jnp.where(turn == 2, -c1, s1))))
            ps.append(top[:, BLOCK:] + jnp.where(turn == 0, s1, jnp.where(turn == 1, c1, jnp.where(turn == 2, -s1, -c1))))
        ends = (lane == 0) & (c == 0)
        re_a = jnp.where(ends, ps[0] + root * (ps[1] - ps[3]), pc[0] + pc[1] + pc[2] + pc[3])
        im_a = -jnp.where(ends, ps[2] + root * (ps[1] + ps[3]), ps[0] + ps[1] + ps[2] + ps[3])
        zero_sine = jnp.where(ends, 0.0, 1.0)
        re_b = pc[0] - pc[2] + zero_sine * (ps[1] - ps[3])
        im_b = pc[3] - pc[1] + zero_sine * (ps[0] - ps[2])
        near = pl.ds(pl.multiple_of(c * BLOCK, BLOCK), BLOCK)
        far = pl.ds(pl.multiple_of(QUARTER + c * BLOCK, BLOCK), BLOCK)
        spec[0, :, near] = re_a
        spec[0, :, far] = re_b
        spec[1, :, near] = im_a
        spec[1, :, far] = im_b
        return total + (re_a * re_a + im_a * im_a) + (re_b * re_b + im_b * im_b)

    total = lax.fori_loop(0, CHUNKS, transform, jnp.zeros((rows, BLOCK), F32))
    for c in range(4):
        inv_copy(c).start()
    level = jnp.sum(total, axis=1, keepdims=True) * (1.0 / NB)
    real_part, imag_part = spec[0], spec[1]
    scale = 1.0 / jnp.sqrt(real_part * real_part + imag_part * imag_part + 0.1 * level + 1e-06)
    result = jnp.concatenate([real_part * scale, imag_part * scale], axis=0).astype(BF16)
    piece = NB // PIECES
    for p in range(PIECES):
        white[0, 0, p] = result[:, p * piece:(p + 1) * piece]

    pl.semaphore_wait(barrier, n)
    even = lax.rem(me, 2) == 0
    odd = lax.rem(me, 2) == 1
    behind = (lax.rem(me + n - 1, n), hour)
    behind2 = (lax.rem(me + n - 2, n), hour)
    ahead = (lax.rem(me + 1, n), hour)
    across = (me, other)

    def near_copy(p, src, dst, kind, device):
        return pltpu.make_async_remote_copy(
            src_ref=white.at[src[0], src[1], p], dst_ref=white.at[dst[0], dst[1], p],
            send_sem=near_send.at[kind, p], recv_sem=near_recv.at[kind, p], device_id=device, device_id_type=MESH,
        )

    def copy_far(p):
        return near_copy(p, (0, 0), (0, 2), 0, behind2)

    def copy_hour(p):
        return near_copy(p, (0, 0), (1, 0), 1, across)

    def copy_both(p):
        return near_copy(p, (0, 2), (1, 2), 2, across) if p % 2 == 0 else near_copy(p, (1, 0), (1, 2), 2, behind2)

    def odd_own(p):
        return near_copy(p, (0, 0), (0, 1), 3, behind)

    def even_own(p):
        return near_copy(p, (0, 2), (0, 1), 3, ahead)

    def odd_other(p):
        return near_copy(p, (1, 0), (1, 1), 4, behind)

    def even_other(p):
        return near_copy(p, (1, 2), (1, 1), 4, ahead)

    for p in range(PIECES):
        copy_far(p).start()
        copy_hour(p).start()

    @pl.when(odd)
    def _():
        for p in range(PIECES):
            odd_own(p).start()

    group = 2 * rows
    wide = lax.broadcasted_iota(jnp.int32, (pairs, 3 * group), 1)
    row_of = lax.broadcasted_iota(jnp.int32, (pairs, pairs), 0)
    column_of = lax.broadcasted_iota(jnp.int32, (pairs, pairs), 1)

    def upright(ref):
        return jnp.sum(jnp.where(row_of == column_of, ref[...], 0), axis=1, keepdims=True)

    first, second = upright(first_ref), upright(second_ref)
    second_base = second // 8 * group + second % 8
    pick_a, pick_b = [], []
    for part in range(2):
        for comp in range(2):
            shift = part * rows + (comp + hour) * 8
            pick_a.append(jnp.where(wide[:, :group] == first + shift, 1.0, 0.0))
        for comp in range(COMPS):
            pick_b.append(jnp.where(wide == second_base + (part * rows + comp * 8), 1.0, 0.0))
    pick_a = jnp.concatenate(pick_a, axis=0).astype(BF16)
    pick_b = jnp.concatenate(pick_b, axis=0).astype(BF16)
    owner_row = owner_ref[...]
    earlier = (upright(owner_ref) == owner_row) & (row_of < column_of)
    place_of = owner_row * 16 + jnp.sum(jnp.where(earlier, 1, 0), axis=0, keepdims=True)
    twice = lax.broadcasted_iota(jnp.int32, (pairs, 2 * pairs), 1) % pairs
    twice = jnp.where(twice == lax.broadcasted_iota(jnp.int32, (pairs, 2 * pairs), 0), 1.0, 0.0).astype(BF16)
    place_of = jnp.broadcast_to(place_of, (8, pairs)).astype(F32).astype(BF16)
    place_of = jnp.dot(place_of, twice, preferred_element_type=F32)[0:1]
    side = lax.broadcasted_iota(jnp.int32, (1, 2 * pairs), 1) // pairs
    target = place_of + (side * 8).astype(F32)
    spot = lax.broadcasted_iota(jnp.int32, (16 * n, 2 * pairs), 0).astype(F32)
    place = jnp.where(spot == target, 1.0, 0.0).astype(BF16)

    step = 256

    def arrive(p):
        copy_far(p).wait_recv()
        if p % 2 == 0:
            copy_both(p).start()

        @pl.when(even)
        def _():
            even_own(p).start()

        copy_hour(p).wait_recv()
        if p % 2 == 1:
            copy_both(p).start()

        @pl.when(odd)
        def _():
            odd_other(p).start()

    def pass_on(p):
        copy_both(p).wait_recv()

        @pl.when(even)
        def _():
            even_other(p).start()

    def correlate(p, h):
        (odd_own, odd_other)[h](p).wait_recv()

        def body(q, carry):
            lanes = pl.ds(pl.multiple_of(q * step, step), step)
            a_v[...] = jnp.dot(pick_a, white[h, 0, p, :, lanes], preferred_element_type=F32).reshape(2, 2, pairs, step)
            b_v[...] = jnp.dot(
                pick_b, white[h, :, p, :, lanes].reshape(3 * group, step), preferred_element_type=F32
            ).reshape(2, COMPS, pairs, step)
            start = p * piece + q * step
            real_lanes = pl.ds(pl.multiple_of(start, step), step)
            imag_lanes = pl.ds(pl.multiple_of(NB + start, step), step)
            for i in range(5):
                kind = hour * 4 + i
                c, e = kind // COMPS - hour, kind % COMPS
                ar, ai, br, bi = a_v[0, c], a_v[1, c], b_v[0, e], b_v[1, e]
                re = ar * br + ai * bi
                im = ar * bi - ai * br
                here = pl.ds(i * pairs, pairs)
                if h == 0:
                    early[here, real_lanes] = re
                    early[here, imag_lanes] = im
                else:
                    cross[here, real_lanes] = (early[here, real_lanes] + re).astype(BF16)
                    cross[here, imag_lanes] = (early[here, imag_lanes] + im).astype(BF16)
            return carry

        lax.fori_loop(0, piece // step, body, 0)

    arrive(0)
    arrive(1)
    correlate(0, 0)
    arrive(2)
    correlate(1, 0)
    arrive(3)
    correlate(2, 0)
    pass_on(0)
    correlate(3, 0)
    pass_on(1)
    correlate(0, 1)
    pass_on(2)
    correlate(1, 1)
    pass_on(3)
    correlate(2, 1)
    correlate(3, 1)

    for c in range(4):
        inv_copy(c).wait()

    spans = (pl.ds(0, 5), pl.ds(5, 4))

    def far_copy(part, source, dst):
        return pltpu.make_async_remote_copy(
            src_ref=outgoing.at[dst, spans[part]], dst_ref=out_ref.at[source, spans[part]],
            send_sem=far_send.at[part, dst], recv_sem=far_recv.at[part, source],
            device_id=(dst, hour), device_id_type=MESH,
        )

    def own_copy(part):
        return pltpu.make_async_copy(outgoing.at[me, spans[part]], out_ref.at[me, spans[part]], own_sem.at[part])

    for part in range(2):
        for lag_half, units, skip in ((hour, ((0, 2, 4), (6, 8))[part], 0), (other, ((1, 3), (5, 7))[part], hour)):
            count = len(units)
            first_row = pl.multiple_of((units[0] // 2 + skip) * pairs, pairs)
            source = cross[pl.ds(first_row, count * pairs), :]
            for side in range(2):
                lagged[side, pl.ds(0, count * pairs)] = jnp.dot(
                    source, inv_v[lag_half * 2 + side], preferred_element_type=F32
                ).astype(BF16)
            for i, unit in enumerate(units):
                both = lagged[:, pl.ds(i * pairs, pairs)].reshape(2 * pairs, 256)
                moved = jnp.dot(place, both, preferred_element_type=F32).astype(BF16)
                outgoing[:, unit] = moved.reshape(n, 16, 256)

        home = me // 8 * 8

        def send(step, carry, part=part):
            far_copy(part, me, lax.rem(home + 8, n) + lax.rem(me + step, 8)).start()

            @pl.when(step > 0)
            def _():
                far_copy(part, me, home + lax.rem(me + step, 8)).start()

            return carry

        lax.fori_loop(0, 8, send, 0)
        own_copy(part).start()

    def finish(step, carry):
        peer = lax.rem(me + step, n)
        for part in range(2):
            copy = far_copy(part, peer, peer)
            copy.wait_send()
            copy.wait_recv()
        return carry

    lax.fori_loop(1, n, finish, 0)
    for part in range(2):
        own_copy(part).wait()
    for p in range(PIECES):
        for copy in (copy_far(p), copy_hour(p), copy_both(p), odd_own(p), odd_other(p)):
            copy.wait_send()


def shards(windows, pair_first, pair_second, owners):
    n = lax.axis_size("sens")
    rows = windows.shape[1] * COMPS
    pairs = pair_first.shape[0]
    fwd, inv = (jnp.asarray(table) for table in folded_tables())
    received = pl.pallas_call(
        functools.partial(kernel, n, pairs),
        out_shape=jax.ShapeDtypeStruct((n, 9, 16, 256), BF16),
        in_specs=[pl.BlockSpec(memory_space=pltpu.HBM)] * 6,
        out_specs=pl.BlockSpec(memory_space=pl.ANY),
        scratch_shapes=[
            pltpu.VMEM((rows, SAMPLES), BF16),
            pltpu.VMEM((1, pairs), jnp.int32),
            pltpu.VMEM((1, pairs), jnp.int32),
            pltpu.VMEM((1, pairs), jnp.int32),
            pltpu.SemaphoreType.DMA((4,)),
            pltpu.VMEM(fwd.shape, BF16),
            pltpu.VMEM(inv.shape, BF16),
            pltpu.VMEM((8 * rows, HALF), BF16),
            pltpu.VMEM((2, rows, NB), F32),
            pltpu.VMEM((2, 3, PIECES, 2 * rows, NB // PIECES), BF16),
            pltpu.VMEM((2, 2, pairs, 256), F32),
            pltpu.VMEM((2, COMPS, pairs, 256), F32),
            pltpu.VMEM((5 * pairs, 2 * NB), F32),
            pltpu.VMEM((5 * pairs, 2 * NB), BF16),
            pltpu.VMEM((2, 3 * pairs, 256), BF16),
            pltpu.VMEM((n, 9, 16, 256), BF16),
            pltpu.SemaphoreType.DMA((CHUNKS,)),
            pltpu.SemaphoreType.DMA((4,)),
            pltpu.SemaphoreType.DMA((5, PIECES)),
            pltpu.SemaphoreType.DMA((5, PIECES)),
            pltpu.SemaphoreType.DMA((2, n)),
            pltpu.SemaphoreType.DMA((2, n)),
            pltpu.SemaphoreType.DMA((2,)),
        ],
        compiler_params=pltpu.CompilerParams(
            collective_id=0, has_side_effects=True, vmem_limit_bytes=56 * 2**20
        ),
    )(
        windows[0].transpose(1, 0, 2).reshape(rows, SAMPLES),
        pair_first[None, :],
        pair_second[None, :],
        owners.reshape(1, pairs),
        fwd,
        inv,
    )
    received = received.reshape(n, 9, 2, 8, 256).transpose(0, 3, 1, 2, 4).reshape(n * 8, WIDTH // 2)
    return received.astype(F32) / jnp.sqrt(F32(2 * NB))


def solution(mesh):
    placed = (P("hour", "sens", None, None), P("sens"), P("sens"), P("sens", None))

    def run(windows, pair_first, pair_second, owners):
        n, hours = mesh.shape["sens"], mesh.shape["hour"]
        pairs = pair_first.shape[0] // n
        fits = hours == 2 and windows.shape[0] == 2 and n == 16 and pairs == 64 and windows.shape[1] == 8 * n
        body = shards if fits else plain_shards
        return jax.shard_map(
            body, mesh=mesh, in_specs=placed, out_specs=P("sens", "hour"), check_vma=False
        )(windows, pair_first, pair_second, owners)

    return run
```

```python
import functools

import jax
import jax.numpy as jnp
import ml_dtypes
import numpy as np
from jax import lax
from jax.experimental import pallas as pl
from jax.experimental.pallas import tpu as pltpu
from jax.sharding import PartitionSpec as P

SAMPLES = 4096
PADDED = 8192
NB = 2048
LAGS = 1024
COMPS = 3
WIDTH = COMPS * COMPS * LAGS
HALF = SAMPLES // 2
QUARTER = NB // 2
BLOCK = 128
CHUNKS = QUARTER // BLOCK
PIECES = 4
MESH = pl.DeviceIdType.MESH
F32 = jnp.float32
BF16 = jnp.bfloat16

def host_tables():
    times = np.arange(HALF, dtype=np.int64)
    bins = np.arange(NB, dtype=np.int64) + 1
    angle = (times[:, None] * bins[None, :] % PADDED) * (2.0 * np.pi / PADDED)
    fwd = np.concatenate([np.cos(angle), -np.sin(angle)], axis=1).astype(ml_dtypes.bfloat16)
    shifts = np.arange(LAGS, dtype=np.int64) - LAGS // 2
    back = (bins[:, None] * shifts[None, :] % PADDED) * (2.0 * np.pi / PADDED)
    inv = np.concatenate([np.cos(back), -np.sin(back)], axis=0).astype(ml_dtypes.bfloat16)
    return fwd, inv


def whiten(rows, fwd):
    count = rows.shape[0]
    both = jnp.concatenate([rows[:, :HALF], rows[:, HALF:]], axis=0)
    spec = jnp.dot(both, fwd, preferred_element_type=jnp.float32)
    ar, ai = spec[:count, :NB], spec[:count, NB:]
    br, bi = spec[count:, :NB], spec[count:, NB:]
    turn = (lax.broadcasted_iota(jnp.int32, (1, NB), 1) + 1) % 4
    even = turn % 2 == 0
    sign_re = jnp.where((turn == 0) | (turn == 1), 1.0, -1.0)
    sign_im = jnp.where((turn == 0) | (turn == 3), 1.0, -1.0)
    real_part = ar + sign_re * jnp.where(even, br, bi)
    imag_part = ai + sign_im * jnp.where(even, bi, br)
    power = real_part * real_part + imag_part * imag_part
    level = jnp.mean(power, axis=1, keepdims=True)
    scale = 1.0 / jnp.sqrt(power + 0.1 * level + 1e-06)
    return jnp.concatenate([real_part * scale, imag_part * scale], axis=1).astype(jnp.bfloat16)


def from_behind(value, axis, steps):
    count = lax.axis_size(axis)
    pairs = [(source, (source + steps) % count) for source in range(count)]
    return lax.ppermute(value, axis, pairs)


def pick(rows, index):
    table = (index[:, None] == jnp.arange(rows.shape[0], dtype=jnp.int32)[None, :]).astype(jnp.bfloat16)
    return jnp.dot(table, rows, preferred_element_type=jnp.float32)


def plain_shards(windows, pair_first, pair_second, owners):
    hours_here, sensors, _, _ = windows.shape
    pairs = pair_first.shape[0]
    hour_count = lax.axis_size("hour")
    owner_count = lax.axis_size("sens")
    hours = hours_here * hour_count
    columns = WIDTH // hour_count
    capacity = max(2, 2 * pairs // owner_count)
    fwd, inv = (jnp.asarray(table) for table in host_tables())

    white = whiten(windows.reshape(hours_here * sensors * COMPS, SAMPLES), fwd)
    white = lax.all_gather(white, "hour", axis=0, tiled=True)
    white = white.reshape(hours, sensors, COMPS * 2 * NB)
    nearer = from_behind(white, "sens", -1)
    farther = from_behind(white, "sens", -2)
    candidates = jnp.concatenate([white, nearer, farther], axis=1)

    start = lax.axis_index("hour") * columns
    first_block = start // LAGS
    blocks = min(COMPS * COMPS, max((h * columns + columns - 1) // LAGS - h * columns // LAGS + 1 for h in range(hour_count)))
    first_block = jnp.minimum(first_block, COMPS * COMPS - blocks)
    kinds = first_block + jnp.arange(blocks, dtype=jnp.int32)

    total_re, total_im = 0.0, 0.0
    for hour in range(hours):
        a = pick(white[hour], pair_first).reshape(pairs, COMPS, 2, NB)
        b = pick(candidates[hour], pair_second).reshape(pairs, COMPS, 2, NB)
        a = jnp.take(a, kinds // COMPS, axis=1)
        b = jnp.take(b, kinds % COMPS, axis=1)
        ar, ai, br, bi = a[:, :, 0], a[:, :, 1], b[:, :, 0], b[:, :, 1]
        total_re = total_re + (ar * br + ai * bi)
        total_im = total_im + (ar * bi - ai * br)
    cross = jnp.concatenate([total_re, total_im], axis=-1).astype(jnp.bfloat16)
    lagged = jnp.dot(cross.reshape(pairs * blocks, 2 * NB), inv, preferred_element_type=jnp.float32)
    lagged = lagged.astype(jnp.bfloat16).reshape(pairs, blocks * LAGS)
    lagged = lax.dynamic_slice_in_dim(lagged, start - first_block * LAGS, columns, axis=1)

    owner = owners[:, 0]
    order = jnp.arange(pairs, dtype=jnp.int32)
    earlier = (owner[:, None] == owner[None, :]) & (order[None, :] < order[:, None])
    target = owner * capacity + jnp.sum(earlier.astype(jnp.int32), axis=1)
    place = (jnp.arange(owner_count * capacity, dtype=jnp.int32)[:, None] == target[None, :]).astype(jnp.bfloat16)
    outgoing = jnp.dot(place, lagged, preferred_element_type=jnp.float32).astype(jnp.bfloat16)
    received = lax.all_to_all(outgoing, "sens", split_axis=0, concat_axis=0, tiled=True)
    return received.astype(jnp.float32) / jnp.sqrt(jnp.float32(NB * hours))


def folded_tables():
    times = np.arange(HALF, dtype=np.int64)
    bins = np.arange(QUARTER, dtype=np.int64)
    angle = (times[:, None] * bins[None, :] % PADDED) * (2.0 * np.pi / PADDED)
    cosine, sine = np.cos(angle), np.sin(angle)
    sine[:, 0] = 1 - 2 * (times // 4 % 2)
    both = np.stack([cosine.reshape(HALF, CHUNKS, BLOCK), sine.reshape(HALF, CHUNKS, BLOCK)], axis=2)
    fwd = both.transpose(1, 0, 2, 3).reshape(CHUNKS, HALF, 2 * BLOCK).astype(ml_dtypes.bfloat16)
    order = np.concatenate([bins, NB - bins])
    order[0] = QUARTER
    shifts = np.arange(LAGS, dtype=np.int64) - LAGS // 2
    back = (order[:, None] * shifts[None, :] % PADDED) * (2.0 * np.pi / PADDED)
    inv = np.concatenate([np.cos(back), -np.sin(back)], axis=0)
    inv = inv.reshape(2 * NB, 4, LAGS // 4).transpose(1, 0, 2).astype(ml_dtypes.bfloat16)
    return fwd, inv


def kernel(
    n, pairs, x_hbm, first_hbm, second_hbm, owner_hbm, fwd_hbm, inv_hbm, out_hbm,
    x_ref, first_ref, second_ref, owner_ref, in_sem, fwd_v, inv_v, xm, spec, white, a_v, b_v, early, cross, lagged, outgoing, landed, stacked,
    fwd_sem, inv_sem, near_send, near_recv, far_send, far_recv, own_sem, out_sem,
):
    me = lax.axis_index("sens")
    hour = lax.axis_index("hour")
    other = 1 - hour

    inputs = [
        pltpu.make_async_copy(source, target, in_sem.at[k])
        for k, (source, target) in enumerate(
            ((x_hbm, x_ref), (first_hbm, first_ref), (second_hbm, second_ref), (owner_hbm, owner_ref))
        )
    ]

    def fwd_copy(c):
        return pltpu.make_async_copy(fwd_hbm.at[c], fwd_v.at[c], fwd_sem.at[c])

    def inv_copy(c):
        return pltpu.make_async_copy(inv_hbm.at[c], inv_v.at[c], inv_sem.at[c])

    for copy in inputs:
        copy.start()
    for c in range(CHUNKS):
        fwd_copy(c).start()

    barrier = pltpu.get_barrier_semaphore()

    def greet(step, carry):
        pl.semaphore_signal(barrier, inc=1, device_id=(lax.rem(me + step, n), hour), device_id_type=MESH)
        return carry

    lax.fori_loop(1, n, greet, 0)
    pl.semaphore_signal(barrier, inc=1, device_id=(me, other), device_id_type=MESH)

    for copy in inputs:
        copy.wait()

    rows = x_ref.shape[0]
    x = x_ref[...].astype(F32)
    halves = jnp.concatenate([x[:, :HALF], x[:, HALF:]], axis=0)
    residue = lax.broadcasted_iota(jnp.int32, (2 * rows, HALF), 1) & 3
    xm[...] = jnp.concatenate([jnp.where(residue == r, halves, 0.0) for r in range(4)], axis=0).astype(BF16)

    lane = lax.broadcasted_iota(jnp.int32, (rows, BLOCK), 1)
    turn = lane & 3
    root = 0.70703125

    def transform(c, total):
        fwd_copy(c).wait()
        part = jnp.dot(xm[...], fwd_v[c], preferred_element_type=F32)
        pc, ps = [], []
        for r in range(4):
            top = part[2 * r * rows:(2 * r + 1) * rows]
            low = part[(2 * r + 1) * rows:(2 * r + 2) * rows]
            c1, s1 = low[:, :BLOCK], low[:, BLOCK:]
            pc.append(top[:, :BLOCK] + jnp.where(turn == 0, c1, jnp.where(turn == 1, -s1, jnp.where(turn == 2, -c1, s1))))
            ps.append(top[:, BLOCK:] + jnp.where(turn == 0, s1, jnp.where(turn == 1, c1, jnp.where(turn == 2, -s1, -c1))))
        ends = (lane == 0) & (c == 0)
        re_a = jnp.where(ends, ps[0] + root * (ps[1] - ps[3]), pc[0] + pc[1] + pc[2] + pc[3])
        im_a = -jnp.where(ends, ps[2] + root * (ps[1] + ps[3]), ps[0] + ps[1] + ps[2] + ps[3])
        zero_sine = jnp.where(ends, 0.0, 1.0)
        re_b = pc[0] - pc[2] + zero_sine * (ps[1] - ps[3])
        im_b = pc[3] - pc[1] + zero_sine * (ps[0] - ps[2])
        near = pl.ds(pl.multiple_of(c * BLOCK, BLOCK), BLOCK)
        far = pl.ds(pl.multiple_of(QUARTER + c * BLOCK, BLOCK), BLOCK)
        spec[0, :, near] = re_a
        spec[0, :, far] = re_b
        spec[1, :, near] = im_a
        spec[1, :, far] = im_b
        return total + (re_a * re_a + im_a * im_a) + (re_b * re_b + im_b * im_b)

    total = lax.fori_loop(0, CHUNKS, transform, jnp.zeros((rows, BLOCK), F32))
    for c in range(4):
        inv_copy(c).start()
    level = jnp.sum(total, axis=1, keepdims=True) * (1.0 / NB)
    real_part, imag_part = spec[0], spec[1]
    scale = 1.0 / jnp.sqrt(real_part * real_part + imag_part * imag_part + 0.1 * level + 1e-06)
    result = jnp.concatenate([real_part * scale, imag_part * scale], axis=0).astype(BF16)
    piece = NB // PIECES
    for p in range(PIECES):
        white[0, 0, p] = result[:, p * piece:(p + 1) * piece]

    pl.semaphore_wait(barrier, n)
    even = lax.rem(me, 2) == 0
    odd = lax.rem(me, 2) == 1
    behind = (lax.rem(me + n - 1, n), hour)
    behind2 = (lax.rem(me + n - 2, n), hour)
    ahead = (lax.rem(me + 1, n), hour)
    across = (me, other)

    def near_copy(p, src, dst, kind, device):
        return pltpu.make_async_remote_copy(
            src_ref=white.at[src[0], src[1], p], dst_ref=white.at[dst[0], dst[1], p],
            send_sem=near_send.at[kind, p], recv_sem=near_recv.at[kind, p], device_id=device, device_id_type=MESH,
        )

    def copy_far(p):
        return near_copy(p, (0, 0), (0, 2), 0, behind2)

    def copy_hour(p):
        return near_copy(p, (0, 0), (1, 0), 1, across)

    def copy_both(p):
        return near_copy(p, (0, 2), (1, 2), 2, across) if p % 2 == 0 else near_copy(p, (1, 0), (1, 2), 2, behind2)

    def odd_own(p):
        return near_copy(p, (0, 0), (0, 1), 3, behind)

    def even_own(p):
        return near_copy(p, (0, 2), (0, 1), 3, ahead)

    def odd_other(p):
        return near_copy(p, (1, 0), (1, 1), 4, behind)

    def even_other(p):
        return near_copy(p, (1, 2), (1, 1), 4, ahead)

    for p in range(PIECES):
        copy_far(p).start()
        copy_hour(p).start()

    @pl.when(odd)
    def _():
        for p in range(PIECES):
            odd_own(p).start()

    group = 2 * rows
    wide = lax.broadcasted_iota(jnp.int32, (pairs, 3 * group), 1)
    row_of = lax.broadcasted_iota(jnp.int32, (pairs, pairs), 0)
    column_of = lax.broadcasted_iota(jnp.int32, (pairs, pairs), 1)

    def upright(ref):
        return jnp.sum(jnp.where(row_of == column_of, ref[...], 0), axis=1, keepdims=True)

    first, second = upright(first_ref), upright(second_ref)
    second_base = second // 8 * group + second % 8
    pick_a, pick_b = [], []
    for part in range(2):
        for comp in range(2):
            shift = part * rows + (comp + hour) * 8
            pick_a.append(jnp.where(wide[:, :group] == first + shift, 1.0, 0.0))
        for comp in range(COMPS):
            pick_b.append(jnp.where(wide == second_base + (part * rows + comp * 8), 1.0, 0.0))
    pick_a = jnp.concatenate(pick_a, axis=0).astype(BF16)
    pick_b = jnp.concatenate(pick_b, axis=0).astype(BF16)
    owner_row = owner_ref[...]
    earlier = (upright(owner_ref) == owner_row) & (row_of < column_of)
    place_of = owner_row * 16 + jnp.sum(jnp.where(earlier, 1, 0), axis=0, keepdims=True)
    twice = lax.broadcasted_iota(jnp.int32, (pairs, 2 * pairs), 1) % pairs
    twice = jnp.where(twice == lax.broadcasted_iota(jnp.int32, (pairs, 2 * pairs), 0), 1.0, 0.0).astype(BF16)
    place_of = jnp.broadcast_to(place_of, (8, pairs)).astype(F32).astype(BF16)
    place_of = jnp.dot(place_of, twice, preferred_element_type=F32)[0:1]
    side = lax.broadcasted_iota(jnp.int32, (1, 2 * pairs), 1) // pairs
    target = place_of + (side * 8).astype(F32)
    spot = lax.broadcasted_iota(jnp.int32, (16 * n, 2 * pairs), 0).astype(F32)
    place = jnp.where(spot == target, 1.0, 0.0).astype(BF16)

    step = 256

    def arrive(p):
        copy_far(p).wait_recv()
        if p % 2 == 0:
            copy_both(p).start()

        @pl.when(even)
        def _():
            even_own(p).start()

        copy_hour(p).wait_recv()
        if p % 2 == 1:
            copy_both(p).start()

        @pl.when(odd)
        def _():
            odd_other(p).start()

    def pass_on(p):
        copy_both(p).wait_recv()

        @pl.when(even)
        def _():
            even_other(p).start()

    def correlate(p, h):
        (odd_own, odd_other)[h](p).wait_recv()

        def body(q, carry):
            lanes = pl.ds(pl.multiple_of(q * step, step), step)
            a_v[...] = jnp.dot(pick_a, white[h, 0, p, :, lanes], preferred_element_type=F32).reshape(2, 2, pairs, step)
            b_v[...] = jnp.dot(
                pick_b, white[h, :, p, :, lanes].reshape(3 * group, step), preferred_element_type=F32
            ).reshape(2, COMPS, pairs, step)
            start = p * piece + q * step
            real_lanes = pl.ds(pl.multiple_of(start, step), step)
            imag_lanes = pl.ds(pl.multiple_of(NB + start, step), step)
            for i in range(5):
                kind = hour * 4 + i
                c, e = kind // COMPS - hour, kind % COMPS
                ar, ai, br, bi = a_v[0, c], a_v[1, c], b_v[0, e], b_v[1, e]
                re = ar * br + ai * bi
                im = ar * bi - ai * br
                here = pl.ds(i * pairs, pairs)
                if h == 0:
                    early[here, real_lanes] = re
                    early[here, imag_lanes] = im
                else:
                    cross[here, real_lanes] = (early[here, real_lanes] + re).astype(BF16)
                    cross[here, imag_lanes] = (early[here, imag_lanes] + im).astype(BF16)
            return carry

        lax.fori_loop(0, piece // step, body, 0)

    arrive(0)
    arrive(1)
    correlate(0, 0)
    arrive(2)
    correlate(1, 0)
    arrive(3)
    correlate(2, 0)
    pass_on(0)
    correlate(3, 0)
    pass_on(1)
    correlate(0, 1)
    pass_on(2)
    correlate(1, 1)
    pass_on(3)
    correlate(2, 1)
    correlate(3, 1)

    for c in range(4):
        inv_copy(c).wait()

    spans = (pl.ds(0, 5), pl.ds(5, 4))

    def far_copy(part, source, dst):
        return pltpu.make_async_remote_copy(
            src_ref=outgoing.at[dst, spans[part]], dst_ref=landed.at[source, spans[part]],
            send_sem=far_send.at[part, dst], recv_sem=far_recv.at[part, source],
            device_id=(dst, hour), device_id_type=MESH,
        )

    def own_copy(part):
        return pltpu.make_async_copy(outgoing.at[me, spans[part]], landed.at[me, spans[part]], own_sem.at[part])

    for part in range(2):
        for lag_half, units, skip in ((hour, ((0, 2, 4), (6, 8))[part], 0), (other, ((1, 3), (5, 7))[part], hour)):
            count = len(units)
            first_row = pl.multiple_of((units[0] // 2 + skip) * pairs, pairs)
            source = cross[pl.ds(first_row, count * pairs), :]
            for side in range(2):
                lagged[side, pl.ds(0, count * pairs)] = jnp.dot(
                    source, inv_v[lag_half * 2 + side], preferred_element_type=F32
                ).astype(BF16)
            for i, unit in enumerate(units):
                both = lagged[:, pl.ds(i * pairs, pairs)].reshape(2 * pairs, 256)
                moved = jnp.dot(place, both, preferred_element_type=F32).astype(BF16)
                outgoing[:, unit] = moved.reshape(n, 16, 256)

        home = me // 8 * 8

        def send(step, carry, part=part):
            far_copy(part, me, lax.rem(home + 8, n) + lax.rem(me + step, 8)).start()

            @pl.when(step > 0)
            def _():
                far_copy(part, me, home + lax.rem(me + step, 8)).start()

            return carry

        lax.fori_loop(0, 8, send, 0)
        own_copy(part).start()

    def out_copy(source):
        here = pl.ds(pl.multiple_of(source * 8, 8), 8)
        return pltpu.make_async_copy(stacked.at[here], out_hbm.at[here], out_sem.at[source])

    def widen(source):
        here = pl.ds(pl.multiple_of(source * 8, 8), 8)
        for unit in range(9):
            both = landed[source, unit].astype(F32) * (1.0 / (2 * NB) ** 0.5)
            stacked[here, unit * 512:unit * 512 + 256] = both[:8]
            stacked[here, unit * 512 + 256:(unit + 1) * 512] = both[8:]
        out_copy(source).start()

    for part in range(2):
        own_copy(part).wait()
    widen(me)

    def finish(step, carry):
        peer = lax.rem(me + step, n)
        for part in range(2):
            far_copy(part, peer, peer).wait_recv()
        widen(peer)
        return carry

    lax.fori_loop(1, n, finish, 0)

    def settle(step, carry):
        peer = lax.rem(me + step, n)
        for part in range(2):
            far_copy(part, peer, peer).wait_send()
        out_copy(peer).wait()
        return carry

    lax.fori_loop(1, n, settle, 0)
    out_copy(me).wait()
    for p in range(PIECES):
        for copy in (copy_far(p), copy_hour(p), copy_both(p), odd_own(p), odd_other(p)):
            copy.wait_send()


def shards(windows, pair_first, pair_second, owners):
    n = lax.axis_size("sens")
    rows = windows.shape[1] * COMPS
    pairs = pair_first.shape[0]
    fwd, inv = (jnp.asarray(table) for table in folded_tables())
    return pl.pallas_call(
        functools.partial(kernel, n, pairs),
        out_shape=jax.ShapeDtypeStruct((8 * n, WIDTH // 2), F32),
        in_specs=[pl.BlockSpec(memory_space=pltpu.HBM)] * 6,
        out_specs=pl.BlockSpec(memory_space=pl.ANY),
        scratch_shapes=[
            pltpu.VMEM((rows, SAMPLES), BF16),
            pltpu.VMEM((1, pairs), jnp.int32),
            pltpu.VMEM((1, pairs), jnp.int32),
            pltpu.VMEM((1, pairs), jnp.int32),
            pltpu.SemaphoreType.DMA((4,)),
            pltpu.VMEM(fwd.shape, BF16),
            pltpu.VMEM(inv.shape, BF16),
            pltpu.VMEM((8 * rows, HALF), BF16),
            pltpu.VMEM((2, rows, NB), F32),
            pltpu.VMEM((2, 3, PIECES, 2 * rows, NB // PIECES), BF16),
            pltpu.VMEM((2, 2, pairs, 256), F32),
            pltpu.VMEM((2, COMPS, pairs, 256), F32),
            pltpu.VMEM((5 * pairs, 2 * NB), F32),
            pltpu.VMEM((5 * pairs, 2 * NB), BF16),
            pltpu.VMEM((2, 3 * pairs, 256), BF16),
            pltpu.VMEM((n, 9, 16, 256), BF16),
            pltpu.VMEM((n, 9, 16, 256), BF16),
            pltpu.VMEM((8 * n, WIDTH // 2), F32),
            pltpu.SemaphoreType.DMA((CHUNKS,)),
            pltpu.SemaphoreType.DMA((4,)),
            pltpu.SemaphoreType.DMA((5, PIECES)),
            pltpu.SemaphoreType.DMA((5, PIECES)),
            pltpu.SemaphoreType.DMA((2, n)),
            pltpu.SemaphoreType.DMA((2, n)),
            pltpu.SemaphoreType.DMA((2,)),
            pltpu.SemaphoreType.DMA((n,)),
        ],
        compiler_params=pltpu.CompilerParams(
            collective_id=0, has_side_effects=True, vmem_limit_bytes=56 * 2**20
        ),
    )(
        windows[0].transpose(1, 0, 2).reshape(rows, SAMPLES),
        pair_first[None, :],
        pair_second[None, :],
        owners.reshape(1, pairs),
        fwd,
        inv,
    )


def solution(mesh):
    placed = (P("hour", "sens", None, None), P("sens"), P("sens"), P("sens", None))

    def run(windows, pair_first, pair_second, owners):
        n, hours = mesh.shape["sens"], mesh.shape["hour"]
        pairs = pair_first.shape[0] // n
        fits = hours == 2 and windows.shape[0] == 2 and n == 16 and pairs == 64 and windows.shape[1] == 8 * n
        body = shards if fits else plain_shards
        return jax.shard_map(
            body, mesh=mesh, in_specs=placed, out_specs=P("sens", "hour"), check_vma=False
        )(windows, pair_first, pair_second, owners)

    return run
```

```python
import functools

import jax
import jax.numpy as jnp
import ml_dtypes
import numpy as np
from jax import lax
from jax.experimental import pallas as pl
from jax.experimental.pallas import tpu as pltpu
from jax.sharding import PartitionSpec as P

SAMPLES = 4096
PADDED = 8192
NB = 2048
LAGS = 1024
COMPS = 3
WIDTH = COMPS * COMPS * LAGS
HALF = SAMPLES // 2
QUARTER = NB // 2
BLOCK = 128
CHUNKS = QUARTER // BLOCK
PIECES = 4
MESH = pl.DeviceIdType.MESH
F32 = jnp.float32
BF16 = jnp.bfloat16

def host_tables():
    times = np.arange(HALF, dtype=np.int64)
    bins = np.arange(NB, dtype=np.int64) + 1
    angle = (times[:, None] * bins[None, :] % PADDED) * (2.0 * np.pi / PADDED)
    fwd = np.concatenate([np.cos(angle), -np.sin(angle)], axis=1).astype(ml_dtypes.bfloat16)
    shifts = np.arange(LAGS, dtype=np.int64) - LAGS // 2
    back = (bins[:, None] * shifts[None, :] % PADDED) * (2.0 * np.pi / PADDED)
    inv = np.concatenate([np.cos(back), -np.sin(back)], axis=0).astype(ml_dtypes.bfloat16)
    return fwd, inv


def whiten(rows, fwd):
    count = rows.shape[0]
    both = jnp.concatenate([rows[:, :HALF], rows[:, HALF:]], axis=0)
    spec = jnp.dot(both, fwd, preferred_element_type=jnp.float32)
    ar, ai = spec[:count, :NB], spec[:count, NB:]
    br, bi = spec[count:, :NB], spec[count:, NB:]
    turn = (lax.broadcasted_iota(jnp.int32, (1, NB), 1) + 1) % 4
    even = turn % 2 == 0
    sign_re = jnp.where((turn == 0) | (turn == 1), 1.0, -1.0)
    sign_im = jnp.where((turn == 0) | (turn == 3), 1.0, -1.0)
    real_part = ar + sign_re * jnp.where(even, br, bi)
    imag_part = ai + sign_im * jnp.where(even, bi, br)
    power = real_part * real_part + imag_part * imag_part
    level = jnp.mean(power, axis=1, keepdims=True)
    scale = 1.0 / jnp.sqrt(power + 0.1 * level + 1e-06)
    return jnp.concatenate([real_part * scale, imag_part * scale], axis=1).astype(jnp.bfloat16)


def from_behind(value, axis, steps):
    count = lax.axis_size(axis)
    pairs = [(source, (source + steps) % count) for source in range(count)]
    return lax.ppermute(value, axis, pairs)


def pick(rows, index):
    table = (index[:, None] == jnp.arange(rows.shape[0], dtype=jnp.int32)[None, :]).astype(jnp.bfloat16)
    return jnp.dot(table, rows, preferred_element_type=jnp.float32)


def plain_shards(windows, pair_first, pair_second, owners):
    hours_here, sensors, _, _ = windows.shape
    pairs = pair_first.shape[0]
    hour_count = lax.axis_size("hour")
    owner_count = lax.axis_size("sens")
    hours = hours_here * hour_count
    columns = WIDTH // hour_count
    capacity = max(2, 2 * pairs // owner_count)
    fwd, inv = (jnp.asarray(table) for table in host_tables())

    white = whiten(windows.reshape(hours_here * sensors * COMPS, SAMPLES), fwd)
    white = lax.all_gather(white, "hour", axis=0, tiled=True)
    white = white.reshape(hours, sensors, COMPS * 2 * NB)
    nearer = from_behind(white, "sens", -1)
    farther = from_behind(white, "sens", -2)
    candidates = jnp.concatenate([white, nearer, farther], axis=1)

    start = lax.axis_index("hour") * columns
    first_block = start // LAGS
    blocks = min(COMPS * COMPS, max((h * columns + columns - 1) // LAGS - h * columns // LAGS + 1 for h in range(hour_count)))
    first_block = jnp.minimum(first_block, COMPS * COMPS - blocks)
    kinds = first_block + jnp.arange(blocks, dtype=jnp.int32)

    total_re, total_im = 0.0, 0.0
    for hour in range(hours):
        a = pick(white[hour], pair_first).reshape(pairs, COMPS, 2, NB)
        b = pick(candidates[hour], pair_second).reshape(pairs, COMPS, 2, NB)
        a = jnp.take(a, kinds // COMPS, axis=1)
        b = jnp.take(b, kinds % COMPS, axis=1)
        ar, ai, br, bi = a[:, :, 0], a[:, :, 1], b[:, :, 0], b[:, :, 1]
        total_re = total_re + (ar * br + ai * bi)
        total_im = total_im + (ar * bi - ai * br)
    cross = jnp.concatenate([total_re, total_im], axis=-1).astype(jnp.bfloat16)
    lagged = jnp.dot(cross.reshape(pairs * blocks, 2 * NB), inv, preferred_element_type=jnp.float32)
    lagged = lagged.astype(jnp.bfloat16).reshape(pairs, blocks * LAGS)
    lagged = lax.dynamic_slice_in_dim(lagged, start - first_block * LAGS, columns, axis=1)

    owner = owners[:, 0]
    order = jnp.arange(pairs, dtype=jnp.int32)
    earlier = (owner[:, None] == owner[None, :]) & (order[None, :] < order[:, None])
    target = owner * capacity + jnp.sum(earlier.astype(jnp.int32), axis=1)
    place = (jnp.arange(owner_count * capacity, dtype=jnp.int32)[:, None] == target[None, :]).astype(jnp.bfloat16)
    outgoing = jnp.dot(place, lagged, preferred_element_type=jnp.float32).astype(jnp.bfloat16)
    received = lax.all_to_all(outgoing, "sens", split_axis=0, concat_axis=0, tiled=True)
    return received.astype(jnp.float32) / jnp.sqrt(jnp.float32(NB * hours))


def folded_tables():
    times = np.arange(HALF, dtype=np.int64)
    bins = np.arange(QUARTER, dtype=np.int64)
    angle = (times[:, None] * bins[None, :] % PADDED) * (2.0 * np.pi / PADDED)
    cosine, sine = np.cos(angle), np.sin(angle)
    sine[:, 0] = 1 - 2 * (times // 4 % 2)
    both = np.stack([cosine.reshape(HALF, CHUNKS, BLOCK), sine.reshape(HALF, CHUNKS, BLOCK)], axis=2)
    fwd = both.transpose(1, 0, 2, 3).reshape(CHUNKS, HALF, 2 * BLOCK).astype(ml_dtypes.bfloat16)
    order = np.concatenate([bins, NB - bins])
    order[0] = QUARTER
    shifts = np.arange(LAGS, dtype=np.int64) - LAGS // 2
    back = (order[:, None] * shifts[None, :] % PADDED) * (2.0 * np.pi / PADDED)
    inv = np.concatenate([np.cos(back), -np.sin(back)], axis=0)
    inv = inv.reshape(2 * NB, 4, LAGS // 4).transpose(1, 0, 2).astype(ml_dtypes.bfloat16)
    return fwd, inv


def kernel(
    n, pairs, x_hbm, first_hbm, second_hbm, owner_hbm, fwd_hbm, inv_hbm, out_ref,
    x_ref, first_ref, second_ref, owner_ref, in_sem, fwd_v, inv_v, xm, spec, white, a_v, b_v, early, cross, lagged, outgoing,
    fwd_sem, inv_sem, near_send, near_recv, far_send, far_recv, own_sem,
):
    me = lax.axis_index("sens")
    hour = lax.axis_index("hour")
    other = 1 - hour

    inputs = [
        pltpu.make_async_copy(source, target, in_sem.at[k])
        for k, (source, target) in enumerate(
            ((x_hbm, x_ref), (first_hbm, first_ref), (second_hbm, second_ref), (owner_hbm, owner_ref))
        )
    ]

    def fwd_copy(c):
        return pltpu.make_async_copy(fwd_hbm.at[c], fwd_v.at[c], fwd_sem.at[c])

    def inv_copy(c):
        return pltpu.make_async_copy(inv_hbm.at[c], inv_v.at[c], inv_sem.at[c])

    for copy in inputs:
        copy.start()
    for c in range(CHUNKS):
        fwd_copy(c).start()

    barrier = pltpu.get_barrier_semaphore()

    def greet(step, carry):
        pl.semaphore_signal(barrier, inc=1, device_id=(lax.rem(me + step, n), hour), device_id_type=MESH)
        return carry

    lax.fori_loop(1, n, greet, 0)
    pl.semaphore_signal(barrier, inc=1, device_id=(me, other), device_id_type=MESH)

    for copy in inputs:
        copy.wait()

    rows = x_ref.shape[0]
    x = x_ref[...].astype(F32)
    halves = jnp.concatenate([x[:, :HALF], x[:, HALF:]], axis=0)
    residue = lax.broadcasted_iota(jnp.int32, (2 * rows, HALF), 1) & 3
    xm[...] = jnp.concatenate([jnp.where(residue == r, halves, 0.0) for r in range(4)], axis=0).astype(BF16)

    lane = lax.broadcasted_iota(jnp.int32, (rows, BLOCK), 1)
    turn = lane & 3
    root = 0.70703125

    def transform(c, total):
        fwd_copy(c).wait()
        part = jnp.dot(xm[...], fwd_v[c], preferred_element_type=F32)
        pc, ps = [], []
        for r in range(4):
            top = part[2 * r * rows:(2 * r + 1) * rows]
            low = part[(2 * r + 1) * rows:(2 * r + 2) * rows]
            c1, s1 = low[:, :BLOCK], low[:, BLOCK:]
            pc.append(top[:, :BLOCK] + jnp.where(turn == 0, c1, jnp.where(turn == 1, -s1, jnp.where(turn == 2, -c1, s1))))
            ps.append(top[:, BLOCK:] + jnp.where(turn == 0, s1, jnp.where(turn == 1, c1, jnp.where(turn == 2, -s1, -c1))))
        ends = (lane == 0) & (c == 0)
        re_a = jnp.where(ends, ps[0] + root * (ps[1] - ps[3]), pc[0] + pc[1] + pc[2] + pc[3])
        im_a = -jnp.where(ends, ps[2] + root * (ps[1] + ps[3]), ps[0] + ps[1] + ps[2] + ps[3])
        zero_sine = jnp.where(ends, 0.0, 1.0)
        re_b = pc[0] - pc[2] + zero_sine * (ps[1] - ps[3])
        im_b = pc[3] - pc[1] + zero_sine * (ps[0] - ps[2])
        near = pl.ds(pl.multiple_of(c * BLOCK, BLOCK), BLOCK)
        far = pl.ds(pl.multiple_of(QUARTER + c * BLOCK, BLOCK), BLOCK)
        spec[0, :, near] = re_a
        spec[0, :, far] = re_b
        spec[1, :, near] = im_a
        spec[1, :, far] = im_b
        return total + (re_a * re_a + im_a * im_a) + (re_b * re_b + im_b * im_b)

    total = lax.fori_loop(0, CHUNKS, transform, jnp.zeros((rows, BLOCK), F32))
    for c in range(4):
        inv_copy(c).start()
    level = jnp.sum(total, axis=1, keepdims=True) * (1.0 / NB)
    real_part, imag_part = spec[0], spec[1]
    scale = 1.0 / jnp.sqrt(real_part * real_part + imag_part * imag_part + 0.1 * level + 1e-06)
    result = jnp.concatenate([real_part * scale, imag_part * scale], axis=0).astype(BF16)
    piece = NB // PIECES
    for p in range(PIECES):
        white[0, 0, p] = result[:, p * piece:(p + 1) * piece]

    pl.semaphore_wait(barrier, n)
    even = lax.rem(me, 2) == 0
    odd = lax.rem(me, 2) == 1
    behind = (lax.rem(me + n - 1, n), hour)
    behind2 = (lax.rem(me + n - 2, n), hour)
    ahead = (lax.rem(me + 1, n), hour)
    across = (me, other)

    def near_copy(p, src, dst, kind, device):
        return pltpu.make_async_remote_copy(
            src_ref=white.at[src[0], src[1], p], dst_ref=white.at[dst[0], dst[1], p],
            send_sem=near_send.at[kind, p], recv_sem=near_recv.at[kind, p], device_id=device, device_id_type=MESH,
        )

    def copy_far(p):
        return near_copy(p, (0, 0), (0, 2), 0, behind2)

    def copy_hour(p):
        return near_copy(p, (0, 0), (1, 0), 1, across)

    def copy_both(p):
        return near_copy(p, (0, 2), (1, 2), 2, across) if p % 2 == 0 else near_copy(p, (1, 0), (1, 2), 2, behind2)

    def odd_own(p):
        return near_copy(p, (0, 0), (0, 1), 3, behind)

    def even_own(p):
        return near_copy(p, (0, 2), (0, 1), 3, ahead)

    def odd_other(p):
        return near_copy(p, (1, 0), (1, 1), 4, behind)

    def even_other(p):
        return near_copy(p, (1, 2), (1, 1), 4, ahead)

    for p in range(PIECES):
        copy_far(p).start()
        copy_hour(p).start()

    @pl.when(odd)
    def _():
        for p in range(PIECES):
            odd_own(p).start()

    group = 2 * rows
    wide = lax.broadcasted_iota(jnp.int32, (pairs, 3 * group), 1)
    row_of = lax.broadcasted_iota(jnp.int32, (pairs, pairs), 0)
    column_of = lax.broadcasted_iota(jnp.int32, (pairs, pairs), 1)

    def upright(ref):
        return jnp.sum(jnp.where(row_of == column_of, ref[...], 0), axis=1, keepdims=True)

    first, second = upright(first_ref), upright(second_ref)
    second_base = second // 8 * group + second % 8
    pick_a, pick_b = [], []
    for part in range(2):
        for comp in range(2):
            shift = part * rows + (comp + hour) * 8
            pick_a.append(jnp.where(wide[:, :group] == first + shift, 1.0, 0.0))
        for comp in range(COMPS):
            pick_b.append(jnp.where(wide == second_base + (part * rows + comp * 8), 1.0, 0.0))
    pick_a = jnp.concatenate(pick_a, axis=0).astype(BF16)
    pick_b = jnp.concatenate(pick_b, axis=0).astype(BF16)
    owner_row = owner_ref[...]
    earlier = (upright(owner_ref) == owner_row) & (row_of < column_of)
    place_of = owner_row * 16 + jnp.sum(jnp.where(earlier, 1, 0), axis=0, keepdims=True)
    twice = lax.broadcasted_iota(jnp.int32, (pairs, 2 * pairs), 1) % pairs
    twice = jnp.where(twice == lax.broadcasted_iota(jnp.int32, (pairs, 2 * pairs), 0), 1.0, 0.0).astype(BF16)
    place_of = jnp.broadcast_to(place_of, (8, pairs)).astype(F32).astype(BF16)
    place_of = jnp.dot(place_of, twice, preferred_element_type=F32)[0:1]
    side = lax.broadcasted_iota(jnp.int32, (1, 2 * pairs), 1) // pairs
    target = place_of + (side * 8).astype(F32)
    spot = lax.broadcasted_iota(jnp.int32, (16 * n, 2 * pairs), 0).astype(F32)
    place = jnp.where(spot == target, 1.0, 0.0).astype(BF16)

    step = 256

    def arrive(p):
        copy_far(p).wait_recv()
        if p % 2 == 0:
            copy_both(p).start()

        @pl.when(even)
        def _():
            even_own(p).start()

        copy_hour(p).wait_recv()
        if p % 2 == 1:
            copy_both(p).start()

        @pl.when(odd)
        def _():
            odd_other(p).start()

    def pass_on(p):
        copy_both(p).wait_recv()

        @pl.when(even)
        def _():
            even_other(p).start()

    def correlate(p, h):
        (odd_own, odd_other)[h](p).wait_recv()

        def body(q, carry):
            lanes = pl.ds(pl.multiple_of(q * step, step), step)
            a_v[...] = jnp.dot(pick_a, white[h, 0, p, :, lanes], preferred_element_type=F32).reshape(2, 2, pairs, step)
            b_v[...] = jnp.dot(
                pick_b, white[h, :, p, :, lanes].reshape(3 * group, step), preferred_element_type=F32
            ).reshape(2, COMPS, pairs, step)
            start = p * piece + q * step
            real_lanes = pl.ds(pl.multiple_of(start, step), step)
            imag_lanes = pl.ds(pl.multiple_of(NB + start, step), step)
            for i in range(5):
                kind = hour * 4 + i
                c, e = kind // COMPS - hour, kind % COMPS
                ar, ai, br, bi = a_v[0, c], a_v[1, c], b_v[0, e], b_v[1, e]
                re = ar * br + ai * bi
                im = ar * bi - ai * br
                here = pl.ds(i * pairs, pairs)
                if h == 0:
                    early[here, real_lanes] = re
                    early[here, imag_lanes] = im
                else:
                    cross[here, real_lanes] = (early[here, real_lanes] + re).astype(BF16)
                    cross[here, imag_lanes] = (early[here, imag_lanes] + im).astype(BF16)
            return carry

        lax.fori_loop(0, piece // step, body, 0)

    arrive(0)
    arrive(1)
    correlate(0, 0)
    arrive(2)
    correlate(1, 0)
    arrive(3)
    correlate(2, 0)
    pass_on(0)
    correlate(3, 0)
    pass_on(1)
    correlate(0, 1)
    pass_on(2)
    correlate(1, 1)
    pass_on(3)
    correlate(2, 1)
    correlate(3, 1)

    for c in range(4):
        inv_copy(c).wait()

    spans = (pl.ds(0, 5), pl.ds(5, 4))

    def far_copy(part, source, dst):
        return pltpu.make_async_remote_copy(
            src_ref=outgoing.at[dst, spans[part]], dst_ref=out_ref.at[source, spans[part]],
            send_sem=far_send.at[part, dst], recv_sem=far_recv.at[part, source],
            device_id=(dst, hour), device_id_type=MESH,
        )

    def own_copy(part):
        return pltpu.make_async_copy(outgoing.at[me, spans[part]], out_ref.at[me, spans[part]], own_sem.at[part])

    for part in range(2):
        for lag_half, units, skip in ((hour, ((0, 2, 4), (6, 8))[part], 0), (other, ((1, 3), (5, 7))[part], hour)):
            count = len(units)
            first_row = pl.multiple_of((units[0] // 2 + skip) * pairs, pairs)
            source = cross[pl.ds(first_row, count * pairs), :]
            for side in range(2):
                lagged[side, pl.ds(0, count * pairs)] = jnp.dot(
                    source, inv_v[lag_half * 2 + side], preferred_element_type=F32
                ).astype(BF16)
            for i, unit in enumerate(units):
                both = lagged[:, pl.ds(i * pairs, pairs)].reshape(2 * pairs, 256)
                moved = jnp.dot(place, both, preferred_element_type=F32).astype(BF16)
                outgoing[:, unit] = moved.reshape(n, 16, 256)

        home = me // 8 * 8

        def send(step, carry, part=part):
            far_copy(part, me, lax.rem(home + 8, n) + lax.rem(me + step, 8)).start()

            @pl.when(step > 0)
            def _():
                far_copy(part, me, home + lax.rem(me + step, 8)).start()

            return carry

        lax.fori_loop(0, 8, send, 0)
        own_copy(part).start()

    def finish(step, carry):
        peer = lax.rem(me + step, n)
        for part in range(2):
            copy = far_copy(part, peer, peer)
            copy.wait_send()
            copy.wait_recv()
        return carry

    lax.fori_loop(1, n, finish, 0)
    for part in range(2):
        own_copy(part).wait()
    for p in range(PIECES):
        for copy in (copy_far(p), copy_hour(p), copy_both(p), odd_own(p), odd_other(p)):
            copy.wait_send()


def shards(windows, pair_first, pair_second, owners):
    n = lax.axis_size("sens")
    rows = windows.shape[1] * COMPS
    pairs = pair_first.shape[0]
    fwd, inv = (jnp.asarray(table) for table in folded_tables())
    received = pl.pallas_call(
        functools.partial(kernel, n, pairs),
        out_shape=jax.ShapeDtypeStruct((n, 9, 16, 256), BF16),
        in_specs=[pl.BlockSpec(memory_space=pltpu.HBM)] * 6,
        out_specs=pl.BlockSpec(memory_space=pltpu.VMEM),
        scratch_shapes=[
            pltpu.VMEM((rows, SAMPLES), BF16),
            pltpu.VMEM((1, pairs), jnp.int32),
            pltpu.VMEM((1, pairs), jnp.int32),
            pltpu.VMEM((1, pairs), jnp.int32),
            pltpu.SemaphoreType.DMA((4,)),
            pltpu.VMEM(fwd.shape, BF16),
            pltpu.VMEM(inv.shape, BF16),
            pltpu.VMEM((8 * rows, HALF), BF16),
            pltpu.VMEM((2, rows, NB), F32),
            pltpu.VMEM((2, 3, PIECES, 2 * rows, NB // PIECES), BF16),
            pltpu.VMEM((2, 2, pairs, 256), F32),
            pltpu.VMEM((2, COMPS, pairs, 256), F32),
            pltpu.VMEM((5 * pairs, 2 * NB), F32),
            pltpu.VMEM((5 * pairs, 2 * NB), BF16),
            pltpu.VMEM((2, 3 * pairs, 256), BF16),
            pltpu.VMEM((n, 9, 16, 256), BF16),
            pltpu.SemaphoreType.DMA((CHUNKS,)),
            pltpu.SemaphoreType.DMA((4,)),
            pltpu.SemaphoreType.DMA((5, PIECES)),
            pltpu.SemaphoreType.DMA((5, PIECES)),
            pltpu.SemaphoreType.DMA((2, n)),
            pltpu.SemaphoreType.DMA((2, n)),
            pltpu.SemaphoreType.DMA((2,)),
        ],
        compiler_params=pltpu.CompilerParams(
            collective_id=0, has_side_effects=True, vmem_limit_bytes=56 * 2**20
        ),
    )(
        windows[0].transpose(1, 0, 2).reshape(rows, SAMPLES),
        pair_first[None, :],
        pair_second[None, :],
        owners.reshape(1, pairs),
        fwd,
        inv,
    )
    received = received.reshape(n, 9, 2, 8, 256).transpose(0, 3, 1, 2, 4).reshape(n * 8, WIDTH // 2)
    return received.astype(F32) / jnp.sqrt(F32(2 * NB))


def solution(mesh):
    placed = (P("hour", "sens", None, None), P("sens"), P("sens"), P("sens", None))

    def run(windows, pair_first, pair_second, owners):
        n, hours = mesh.shape["sens"], mesh.shape["hour"]
        pairs = pair_first.shape[0] // n
        fits = hours == 2 and windows.shape[0] == 2 and n == 16 and pairs == 64 and windows.shape[1] == 8 * n
        body = shards if fits else plain_shards
        return jax.shard_map(
            body, mesh=mesh, in_specs=placed, out_specs=P("sens", "hour"), check_vma=False
        )(windows, pair_first, pair_second, owners)

    return run
```
